128 devices in a mesh: ha: 8 (over y, x_lo), ta: 16 (over z, x_hi, core).
Axes of the slice: x: 4 (x_hi: 2, x_lo: 2; x = x_hi * 2 + x_lo), y: 4, z: 4, core: 2. Of those that a mesh axis runs over, the one named last changes fastest.
Arguments:
- latent: bfloat16 [32, 64, 128, 512], P('ta', 'ha'), may hold values from -6 to 6
- w_first: bfloat16 [512, 512], replicated, may hold values from -0.25 to 0.25
- w_second: bfloat16 [512, 512], replicated, may hold values from -0.25 to 0.25
- kernel: bfloat16 [2, 3, 3, 128, 128], replicated, may hold values from -0.125 to 0.125
- cotangent: bfloat16 [32, 128, 256, 128], P('ta', 'ha'), may hold values from -6 to 6
Outputs:
- grad_latent: bfloat16 [32, 64, 128, 512], P('ta', 'ha')
- grad_first: float32 [512, 512], replicated
- grad_second: float32 [512, 512], replicated
- grad_kernel: float32 [2, 3, 3, 128, 128], replicated
The draws below stay inside these ranges and needn't reach their ends.
All inputs are finite; a program needn't handle non-finite values.
Results may differ from the reference program's by a relative error of at most 0.012.
Values may be sent and summed in bfloat16 or wider, within the bound.
No kernel may reach another device: no remote copies, remote signals or barrier semaphores. Data moves between devices by JAX's collectives and lax.ppermute only.
A program may use at most 192 MiB of HBM per device.

```python
import jax
import jax.numpy as jnp
from jax import lax

C = 128
LATENT = 512
MID = 512
COLS = 256
FRAMES = 32
HEIGHT = 128
HC = 64
WC = 128


def level_of(rng, shape, cuts, least, high):
    level, own = 1.0, jax.random.fold_in(rng, 6)
    for position, blocks in cuts:
        heights = jnp.exp(jax.random.uniform(jax.random.fold_in(own, position), (blocks,), jnp.float32, least / len(cuts), high / len(cuts)))
        level = level * jnp.repeat(heights, shape[position] // blocks).reshape([-1 if axis == position else 1 for axis in range(len(shape))])
    return level


def scatter_about(own_key, shape, scale, limit, shards=(), kind=jnp.bfloat16):
    loudness = level_of(own_key, shape, shards, -0.22, 0.18) if shards else 1.0
    drawn = jax.random.normal(own_key, shape, jnp.float32) * scale * loudness
    return jnp.minimum(jnp.maximum(drawn, -limit), limit).astype(kind)


def setup_inputs(seed: int = 0) -> dict:
    seeds = jax.random.split(jax.random.key(seed), 6)
    latent = scatter_about(seeds[0], (FRAMES, HC, WC, LATENT), 1.0, 6.0, ((0, 16), (1, 8)))
    w_first = scatter_about(seeds[1], (LATENT, MID), LATENT ** -0.5, 0.25)
    w_second = scatter_about(seeds[2], (MID, LATENT), MID ** -0.5, 0.25)
    kernel = scatter_about(seeds[3], (2, 3, 3, C, C), (18 * C) ** -0.5, 0.125)
    cotangent = scatter_about(seeds[4], (FRAMES, HEIGHT, COLS, C), 1.0, 6.0, ((0, 16), (1, 8)))
    return dict(latent=latent, w_first=w_first, w_second=w_second, kernel=kernel, cotangent=cotangent)


def synthesize(mixed):
    frames, rows, cols, width = mixed.shape
    bands = mixed.astype(jnp.float32).reshape(frames, rows, cols, 4, width // 4)
    low_low, low_high, high_low, high_high = bands[:, :, :, 0], bands[:, :, :, 1], bands[:, :, :, 2], bands[:, :, :, 3]
    top_left = 0.5 * (low_low + low_high + high_low + high_high)
    top_right = 0.5 * (low_low + low_high - high_low - high_high)
    low_left = 0.5 * (low_low - low_high + high_low - high_high)
    low_right = 0.5 * (low_low - low_high - high_low + high_high)
    upper = jnp.stack([top_left, top_right], axis=3)
    lower = jnp.stack([low_left, low_right], axis=3)
    whole = jnp.stack([upper, lower], axis=2)
    return whole.reshape(frames, 2 * rows, 2 * cols, width // 4)


def analyze(grad_fine):
    frames, rows, cols, chans = grad_fine.shape
    split = grad_fine.astype(jnp.float32).reshape(frames, rows // 2, 2, cols // 2, 2, chans)
    aa, bb, cc, dd = split[:, :, 0, :, 0], split[:, :, 0, :, 1], split[:, :, 1, :, 0], split[:, :, 1, :, 1]
    return jnp.concatenate([0.5 * (aa + bb + cc + dd), 0.5 * (aa + bb - cc - dd), 0.5 * (aa - bb + cc - dd), 0.5 * (aa - bb - cc + dd)], axis=-1)


def silu_slope(pre):
    sig = jax.nn.sigmoid(pre)
    return sig * (1.0 + pre * (1.0 - sig))


def conv_backward(fine_pad, grad_pad, cotangent, kernel):
    frames, rows, cols, chans = cotangent.shape
    flat_grad = cotangent.reshape(-1, chans)
    total = cotangent.astype(jnp.float32)
    taps = []
    for dt in range(2):
        for dy in range(3):
            for dx in range(3):
                window = fine_pad[dt:dt + frames, dy:dy + rows, dx:dx + cols].reshape(-1, chans)
                taps.append(lax.dot_general(window, flat_grad, (((0,), (0,)), ((), ())), preferred_element_type=jnp.float32))
                back = grad_pad[1 - dt:1 - dt + frames, 2 - dy:2 - dy + rows, 2 - dx:2 - dx + cols].reshape(-1, chans)
                total = total + jnp.dot(back, kernel[dt, dy, dx].T, preferred_element_type=jnp.float32).reshape(frames, rows, cols, chans)
    return jnp.stack(taps).reshape(2, 3, 3, chans, chans), total.astype(jnp.bfloat16)


def reference(latent, w_first, w_second, kernel, cotangent):
    width = latent.shape[-1]
    flat = latent.reshape(-1, width)
    pre = jnp.dot(flat, w_first, preferred_element_type=jnp.float32)
    act = jax.nn.silu(pre).astype(jnp.bfloat16)
    mixed = (flat.astype(jnp.float32) + jnp.dot(act, w_second, preferred_element_type=jnp.float32)).astype(jnp.bfloat16)
    fine = synthesize(mixed.reshape(latent.shape)).astype(jnp.bfloat16)
    fine_pad = jnp.pad(fine, ((1, 0), (1, 1), (1, 1), (0, 0)))
    grad_pad = jnp.pad(cotangent, ((0, 1), (1, 1), (1, 1), (0, 0)))
    grad_kernel, grad_fine = conv_backward(fine_pad, grad_pad, cotangent, kernel)
    grad_mixed = analyze(grad_fine).astype(jnp.bfloat16).reshape(-1, width)
    slope = jnp.dot(grad_mixed, w_second.T, preferred_element_type=jnp.float32)
    grad_pre = (slope * silu_slope(pre)).astype(jnp.bfloat16)
    grad_latent = (grad_mixed.astype(jnp.float32) + jnp.dot(grad_pre, w_first.T, preferred_element_type=jnp.float32)).astype(jnp.bfloat16)
    grad_first = lax.dot_general(flat, grad_pre, (((0,), (0,)), ((), ())), preferred_element_type=jnp.float32)
    grad_second = lax.dot_general(act, grad_mixed, (((0,), (0,)), ((), ())), preferred_element_type=jnp.float32)
    return grad_latent.reshape(latent.shape), grad_first, grad_second, grad_kernel
```

```python
import functools
import jax
import jax.numpy as jnp
from jax import lax
from jax.experimental import pallas as pl
from jax.experimental.pallas import tpu as pltpu
from jax.sharding import PartitionSpec as P

BF, F32 = jnp.bfloat16, jnp.float32


def dot(a, b):
    return jnp.dot(a, b, preferred_element_type=F32)


def forward_kernel(x_ref, w1_ref, w2_ref, k_ref, act_ref, slope_ref, ft_ref, taps_ref, w1t_ref, w2t_ref):
    @pl.when(pl.program_id(0) == 0)
    def _():
        w1t_ref[...] = w1_ref[...].T
        w2t_ref[...] = w2_ref[...].T
        taps_ref[...] = jnp.zeros_like(taps_ref)
        for t in range(6):
            for dx in range(3):
                tap = k_ref[3 * t + dx].T
                for q in range(2):
                    col = 2 - dx + q
                    taps_ref[t, 128 * col : 128 * (col + 1), 128 * q : 128 * (q + 1)] = tap

    x = x_ref[...]
    pre = dot(x, w1_ref[...])
    sig = 0.5 * jnp.tanh(0.5 * pre) + 0.5
    act = pre * sig
    slope_ref[...] = (sig + act * (1.0 - sig)).astype(BF)
    act = act.astype(BF)
    act_ref[...] = act
    mixed = 0.5 * (x.astype(F32) + dot(act, w2_ref[...]))
    ll, lh, hl, hh = (mixed[:, 128 * b : 128 * (b + 1)] for b in range(4))
    s, d, t, u = ll + lh, ll - lh, hl + hh, hl - hh
    for i in range(x.shape[0] // 128):
        px = slice(128 * i, 128 * (i + 1))
        for p, (m, n) in enumerate(((s, t), (d, u))):
            row = 2 * i + p
            lanes = slice(128 * row, 128 * (row + 1))
            ft_ref[0, 0:128, lanes] = (m[px] + n[px]).astype(BF).T
            ft_ref[0, 128:256, lanes] = (m[px] - n[px]).astype(BF).T


def forward(latent, w1, w2, kernel, rows=256):
    n = latent.shape[0]
    steps = n // rows
    per = steps // 2
    sds = jax.ShapeDtypeStruct
    full = lambda *s: pl.BlockSpec(s, lambda i: (0,) * len(s))
    return pl.pallas_call(
        forward_kernel,
        grid=(steps,),
        in_specs=[
            pl.BlockSpec((rows, 512), lambda i: (i, 0)),
            full(512, 512),
            full(512, 512),
            full(18, 128, 128),
        ],
        out_specs=[
            pl.BlockSpec((rows, 512), lambda i: (i, 0)),
            pl.BlockSpec((rows, 512), lambda i: (i, 0)),
            pl.BlockSpec((1, 256, 2 * rows), lambda i: (i // per, 0, i % per)),
            full(6, 512, 256),
            full(512, 512),
            full(512, 512),
        ],
        out_shape=[
            sds((n, 512), BF),
            sds((n, 512), BF),
            sds((2, 256, n), BF),
            sds((6, 512, 256), BF),
            sds((512, 512), BF),
            sds((512, 512), BF),
        ],
        compiler_params=pltpu.CompilerParams(vmem_limit_bytes=32 << 20),
    )(latent, w1, w2, kernel.reshape(18, 128, 128))


ROWS = 16


def half_kernel(frame, first, *refs):
    refs = list(refs)
    take = lambda n: [refs.pop(0) for _ in range(n)]
    cot_h, above_h, below_h = take(3)
    cot_a, above_a, below_a = cot_h.at[frame], above_h.at[frame], below_h.at[frame]
    if first:
        cot_b, above_b, below_b = cot_h.at[1], above_h.at[1], below_h.at[1]
    else:
        later_h, edges_h = take(2)
        cot_b, above_b, below_b = later_h.at[0], edges_h.at[0], edges_h.at[1]
    lat_h, act_h, slope_h, ft_h, taps_h, w1t_h, w2t_h = take(7)
    if first:
        gl_h, gk_h, gw_h = take(3)
    else:
        sumk_h, sumw_h, _, ids = take(4)
        gl_h, keep_h, send_h = take(3)
    cells, spread, planes, lat, act, slope, ft, taps, w1t, w2t, gm, gp, gl, gk, gw, sems = take(16)
    n_px = lat.shape[0]
    base = frame * n_px
    px = pl.ds(base, n_px)
    copies = {}

    def fetch(name, k, src, dst):
        c = pltpu.make_async_copy(src, dst, sems.at[k])
        c.start()
        copies[name] = c

    fetch("a", 0, cot_a, cells.at[0, pl.ds(1, ROWS)])
    fetch("a0", 1, above_a, cells.at[0, 0])
    fetch("a1", 2, below_a, cells.at[0, ROWS + 1])
    fetch("b", 3, cot_b, cells.at[1, pl.ds(1, ROWS)])
    fetch("b0", 4, above_b, cells.at[1, 0])
    fetch("b1", 5, below_b, cells.at[1, ROWS + 1])
    fetch("taps", 6, taps_h, taps)
    fetch("w2t", 7, w2t_h, w2t)
    fetch("slope", 8, slope_h.at[px], slope)
    fetch("w1t", 9, w1t_h, w1t)
    fetch("ft", 10, ft_h.at[frame], ft.at[:, pl.ds(128, ROWS * 128)])
    fetch("lat", 11, lat_h.at[px], lat)
    fetch("act", 12, act_h.at[px], act)
    if not first:
        fetch("gk", 13, sumk_h, gk)
        fetch("gw", 14, sumw_h, gw)

    zero = jnp.zeros((8, 128), F32)
    for s in range(spread.shape[0]):
        spread[s, 0:8, :] = zero
        spread[s, 264:272, :] = zero
    ft[:, 0:128] = jnp.zeros((256, 128), BF)
    ft[:, 128 * (ROWS + 1) : 128 * (ROWS + 2)] = jnp.zeros((256, 128), BF)

    def split(b):
        def body(r, carry):
            for s in range(2):
                row = 2 * r + s
                spread[s, 8:264, :] = cells[b, row].astype(F32)
                for c in range(4):
                    planes[b, row, :, 128 * c : 128 * (c + 1)] = spread[
                        s, pl.ds(7 + c, 128, stride=2), :
                    ].astype(BF)
            return carry

        lax.fori_loop(0, ROWS // 2 + 1, body, 0)

    for name in ("a", "a0", "a1"):
        copies[name].wait()
    split(0)
    for name in ("b", "b0", "b1"):
        copies[name].wait()
    split(1)
    for name in ("taps", "w2t", "slope", "w1t"):
        copies[name].wait()
    step = 4

    def back(k, carry):
        y = k * step
        total = planes[0, pl.ds(y + 1, step), :, 128:384].reshape(step * 128, 256).astype(F32)
        for dt in range(2):
            for dy in range(3):
                window = planes[1 - dt, pl.ds(y + 2 - dy, step)].reshape(step * 128, 512)
                total = total + dot(window, taps[3 * dt + dy])
        total = (0.5 * total).reshape(step // 2, 2, 128, 256)
        upper = total[:, 0].reshape(step * 64, 256)
        lower = total[:, 1].reshape(step * 64, 256)
        a, b, c, d = upper[:, :128], upper[:, 128:], lower[:, :128], lower[:, 128:]
        ab, am, cd, cm = a + b, a - b, c + d, c - d
        grad = jnp.concatenate([ab + cd, ab - cd, am + cm, am - cm], axis=1).astype(BF)
        here = pl.ds(pl.multiple_of(k * step * 64, step * 64), step * 64)
        gm[here] = grad
        hidden = (dot(grad, w2t[...]) * slope[here].astype(F32)).astype(BF)
        gp[here] = hidden
        gl[here] = (grad.astype(F32) + dot(hidden, w1t[...])).astype(BF)
        return carry

    lax.fori_loop(0, ROWS // step, back, 0)
    out = pltpu.make_async_copy(gl, gl_h.at[px], sems.at[15])
    out.start()
    copies["ft"].wait()
    if not first:
        copies["gk"].wait()
    for b in range(2):
        cols = planes[b].reshape((ROWS + 2) * 128, 512)
        for dy in range(3):
            t = 3 * (1 - b) + dy
            got = dot(ft[:, 128 : 128 * (ROWS + 1)], cols[128 * (2 - dy) : 128 * (ROWS + 2 - dy)])
            for dx in range(3):
                col = 2 - dx
                both = got[0:128, 128 * col : 128 * (col + 1)] + got[128:256, 128 * (col + 1) : 128 * (col + 2)]
                where = slice(128 * (3 * t + dx), 128 * (3 * t + dx + 1))
                if first:
                    gk[where] = both
                else:
                    gk[where] += both
    for name in ("lat", "act"):
        copies[name].wait()
    if not first:
        copies["gw"].wait()
    for n, (left, right) in enumerate(((lat, gp), (act, gm))):
        for m in range(2):
            part = lax.dot_general(
                left[:, 256 * m : 256 * (m + 1)], right[...], (((0,), (0,)), ((), ())), preferred_element_type=F32
            )
            where = slice(512 * n + 256 * m, 512 * n + 256 * (m + 1))
            if first:
                gw[where] = part
            else:
                gw[where] += part
    if first:
        last = [pltpu.make_async_copy(gk, gk_h, sems.at[0]), pltpu.make_async_copy(gw, gw_h, sems.at[1])]
    else:
        (packed,) = take(1)
        for r in range(8):
            b = ids[r]
            for lane in range(4):
                packed[r, 128 * lane : 128 * (lane + 1), :] = gw[
                    pl.ds(pl.multiple_of(b * 128, 128), 128), 128 * lane : 128 * (lane + 1)
                ].astype(BF)
            packed[r, 512:800, :] = gk[pl.ds(pl.multiple_of(b * 288, 32), 288), :].astype(BF)
        last = [
            pltpu.make_async_copy(packed.at[0:4], keep_h, sems.at[0]),
            pltpu.make_async_copy(packed.at[4:8], send_h, sems.at[1]),
        ]
    for c in last:
        c.start()
    for c in last:
        c.wait()
    out.wait()


def half(frame, cells, rest, sums=None):
    first = sums is None
    n = rest[0].shape[0]
    n_px = n // 2
    sds = jax.ShapeDtypeStruct
    any_ = pl.BlockSpec(memory_space=pl.ANY)
    ops = list(cells) + list(rest)
    specs = [any_] * len(ops)
    alias = {}
    packed = []
    if first:
        shapes = [sds((n, 512), BF), sds((2304, 128), F32), sds((1024, 512), F32)]
    else:
        alias = {len(ops) + 2: 0}
        ops += list(sums)
        specs += [any_] * 3 + [pl.BlockSpec(memory_space=pltpu.SMEM)]
        shapes = [sds((n, 512), BF), sds((4, 800, 128), BF), sds((4, 800, 128), BF)]
        packed = [pltpu.VMEM((8, 800, 128), BF)]
    return pl.pallas_call(
        functools.partial(half_kernel, frame, first),
        in_specs=specs,
        out_specs=[any_] * 3,
        out_shape=shapes,
        input_output_aliases=alias,
        scratch_shapes=[
            pltpu.VMEM((2, ROWS + 2, 256, 128), BF),
            pltpu.VMEM((2, 272, 128), F32),
            pltpu.VMEM((2, ROWS + 2, 128, 512), BF),
            pltpu.VMEM((n_px, 512), BF),
            pltpu.VMEM((n_px, 512), BF),
            pltpu.VMEM((n_px, 512), BF),
            pltpu.VMEM((256, (ROWS + 2) * 128), BF),
            pltpu.VMEM((6, 512, 256), BF),
            pltpu.VMEM((512, 512), BF),
            pltpu.VMEM((512, 512), BF),
            pltpu.VMEM((n_px, 512), BF),
            pltpu.VMEM((n_px, 512), BF),
            pltpu.VMEM((n_px, 512), BF),
            pltpu.VMEM((2304, 128), F32),
            pltpu.VMEM((1024, 512), F32),
            pltpu.SemaphoreType.DMA((16,)),
        ]
        + packed,
        compiler_params=pltpu.CompilerParams(vmem_limit_bytes=48 << 20),
    )(*ops)


def unpack_kernel(ids, own, near, far, last, other, gw_ref, gk_ref):
    for r in range(8):
        b = ids[r]
        piece = (own, near, far, last)[r] if r < 4 else other.at[r - 4]
        for lane in range(4):
            gw_ref[pl.ds(pl.multiple_of(b * 128, 128), 128), 128 * lane : 128 * (lane + 1)] = piece[
                128 * lane : 128 * (lane + 1), :
            ].astype(F32)
        gk_ref[pl.ds(pl.multiple_of(b * 288, 32), 288), :] = piece[512:800, :].astype(F32)


def unpack(ids, *pieces):
    vmem = pl.BlockSpec(memory_space=pltpu.VMEM)
    return pl.pallas_call(
        unpack_kernel,
        in_specs=[pl.BlockSpec(memory_space=pltpu.SMEM)] + [vmem] * 5,
        out_specs=[vmem] * 2,
        out_shape=[jax.ShapeDtypeStruct((1024, 512), F32), jax.ShapeDtypeStruct((2304, 128), F32)],
        compiler_params=pltpu.CompilerParams(vmem_limit_bytes=32 << 20),
    )(ids, *pieces)


BOTH = ("ha", "ta")


def coords(device):
    ha, ta = divmod(device, 16)
    return [(ta // 2 % 2) * 2 + ha % 2, ha // 2, ta // 4, ta % 2]


def device_at(x, y, z, core):
    return (y * 2 + x % 2) * 16 + z * 4 + (x // 2) * 2 + core


def along(axes, step):
    pairs = []
    for device in range(128):
        place = coords(device)
        axis = axes[place[3]]
        place[axis] = (place[axis] + step) % 4
        pairs.append((device, device_at(*place)))
    return pairs


def rounded(value):
    return lax.reduce_precision(value, 8, 7).astype(BF)


def swap(value):
    return lax.ppermute(value, BOTH, [(i, i ^ 1) for i in range(128)])


def trade(near, far, last, axes):
    across = lax.ppermute(far, BOTH, along(axes, 2))
    before = lax.ppermute(near, BOTH, along(axes, 1))
    after = lax.ppermute(last, BOTH, along(axes, 3))
    return before, across, after


def add4(own, before, across, after):
    return rounded((own.astype(F32) + across.astype(F32)) + (before.astype(F32) + after.astype(F32)))


def block_ids():
    ha, ta = lax.axis_index("ha"), lax.axis_index("ta")
    core = ta % 2
    x, y = (ta // 2 % 2) * 2 + ha % 2, ha // 2
    ids = []
    for other in range(2):
        owner = core ^ other
        start = jnp.where(owner == 0, x, y)
        ids += [owner * 4 + (start + k) % 4 for k in range(4)]
    return jnp.stack(ids).astype(jnp.int32)


def sum_all(keep, send):
    got = swap(send)
    parts = [rounded(keep[k].astype(F32) + got[k].astype(F32)) for k in range(4)]
    own = add4(parts[0], *trade(*parts[1:], (0, 1)))
    own = add4(own, *trade(own, own, own, (1, 2)))
    own = add4(own, *trade(own, own, own, (2, 0)))
    before, across, after = trade(own, own, own, (0, 1))
    other = swap(jnp.stack([own, after, across, before]))
    return own, after, across, before, other


def neighbour(value, axis, step):
    count = lax.axis_size(axis)
    return lax.ppermute(value, axis, [(i, i + step) for i in range(count) if 0 <= i + step < count])


def shards(latent, w_first, w_second, kernel, cotangent):
    width = latent.shape[-1]
    flat = latent.reshape(-1, width)
    later = neighbour(cotangent[:1], "ta", -1)
    above = neighbour(cotangent[:, -1], "ha", 1)
    below = neighbour(cotangent[:, 0], "ha", -1)
    act, slope, fine, taps, w1t, w2t = forward(flat, w_first, w_second, kernel)
    edges = neighbour(jnp.stack([above[0], below[0]]), "ta", -1)
    rest = (flat, act, slope, fine, taps, w1t, w2t)
    ids = block_ids()
    grad, gk, gw = half(0, (cotangent, above, below), rest)
    grad, keep, send = half(1, (cotangent, above, below, later, edges), rest, (gk, gw, grad, ids))
    gw, gk = unpack(ids, *sum_all(keep, send))
    return grad.reshape(latent.shape), gw[:512], gw[512:], gk.reshape(kernel.shape)


def solution(mesh):
    return jax.shard_map(
        shards,
        mesh=mesh,
        in_specs=(P("ta", "ha", None, None), P(), P(), P(), P("ta", "ha", None, None)),
        out_specs=(P("ta", "ha", None, None), P(), P(), P()),
        check_vma=False,
    )
```

```python
import functools
import jax
import jax.numpy as jnp
from jax import lax
from jax.experimental import pallas as pl
from jax.experimental.pallas import tpu as pltpu
from jax.sharding import PartitionSpec as P

BF, F32 = jnp.bfloat16, jnp.float32
ROWS = 16
MIB = 1 << 20


def in_hbm(*arrays):
    return [pltpu.with_memory_space_constraint(array, pltpu.HBM) for array in arrays]


def in_vmem(*arrays):
    return [pltpu.with_memory_space_constraint(array, pltpu.VMEM) for array in arrays]


def dot(a, b):
    return jnp.dot(a, b, preferred_element_type=F32)


CHUNK = 512


def forward_kernel(lat_h, w1_h, w2_h, k_h, cot_h, *refs):
    lat, act, slope, ft, taps, w1t, w2t, cot_a, cot_b, w1, w2, ker, sems = refs
    chunks = lat.shape[0] // CHUNK
    weights = [
        pltpu.make_async_copy(src, dst, sems.at[n])
        for n, (src, dst) in enumerate(((w1_h, w1), (w2_h, w2), (k_h, ker)))
    ]
    frames = [
        pltpu.make_async_copy(cot_h.at[n], dst.at[pl.ds(1, ROWS)], sems.at[3 + n])
        for n, dst in enumerate((cot_a, cot_b))
    ]

    def pixels(k):
        where = pl.ds(k * CHUNK, CHUNK)
        return pltpu.make_async_copy(lat_h.at[where], lat.at[where], sems.at[5 + k])

    weights[0].start()
    pixels(0).start()
    weights[1].start()
    for k in range(1, chunks):
        pixels(k).start()
    weights[2].start()
    for copy in frames:
        copy.start()
    weights[0].wait()
    pixels(0).wait()
    weights[1].wait()

    for k in range(chunks):
        if k:
            pixels(k).wait()
        here = slice(k * CHUNK, (k + 1) * CHUNK)
        x = lat[here]
        pre = dot(x, w1[...])
        sig = 0.5 * jnp.tanh(0.5 * pre) + 0.5
        hidden = pre * sig
        slope[here] = (sig + hidden * (1.0 - sig)).astype(BF)
        hidden = hidden.astype(BF)
        act[here] = hidden
        mixed = 0.5 * (x.astype(F32) + dot(hidden, w2[...]))
        ll, lh, hl, hh = (mixed[:, 128 * b : 128 * (b + 1)] for b in range(4))
        s, d, t, u = ll + lh, ll - lh, hl + hh, hl - hh
        for i in range(CHUNK // 128):
            px = slice(128 * i, 128 * (i + 1))
            for p, (m, n) in enumerate(((s, t), (d, u))):
                row = 2 * (k * CHUNK // 128 + i) + p
                frame, row = row // ROWS, row % ROWS
                lanes = slice(128 * row, 128 * (row + 1))
                ft[frame, 0:128, lanes] = (m[px] + n[px]).astype(BF).T
                ft[frame, 128:256, lanes] = (m[px] - n[px]).astype(BF).T
    w1t[...] = w1[...].T
    w2t[...] = w2[...].T
    weights[2].wait()
    for t in range(6):
        for q in range(2):
            col = 3 * (1 - q)
            taps[t, 128 * col : 128 * (col + 1), 128 * q : 128 * (q + 1)] = jnp.zeros((128, 128), BF)
        for dx in range(3):
            tap = ker[3 * t + dx].T
            for q in range(2):
                col = 2 - dx + q
                taps[t, 128 * col : 128 * (col + 1), 128 * q : 128 * (q + 1)] = tap
    for copy in frames:
        copy.wait()


def forward(latent, w1, w2, kernel, cotangent):
    n = latent.shape[0]
    frame = (ROWS + 2,) + cotangent.shape[2:]
    vmem = pl.BlockSpec(memory_space=pltpu.VMEM)
    shapes = [(n, 512), (n, 512), (n, 512), (2, 256, n), (6, 512, 256), (512, 512), (512, 512), frame, frame]
    return pl.pallas_call(
        forward_kernel,
        in_specs=[pl.BlockSpec(memory_space=pl.ANY)] * 5,
        out_specs=[vmem] * len(shapes),
        out_shape=[pltpu.VMEM(shape, BF) for shape in shapes],
        scratch_shapes=[
            pltpu.VMEM((512, 512), BF),
            pltpu.VMEM((512, 512), BF),
            pltpu.VMEM((18, 128, 128), BF),
            pltpu.SemaphoreType.DMA((5 + n // CHUNK,)),
        ],
        cost_estimate=pl.CostEstimate(flops=8 * n * 512 * 512, bytes_accessed=12 * MIB, transcendentals=n * 512),
        compiler_params=pltpu.CompilerParams(vmem_limit_bytes=16 * MIB),
    )(*in_hbm(latent, w1, w2, kernel.reshape(18, 128, 128), cotangent))


def border_kernel(first, second, _, __, cot_a, cot_b):
    odd = lax.axis_index("ha") % 2
    for upper, lower, here in ((second, first, odd == 0), (first, second, odd == 1)):

        @pl.when(here)
        def _():
            for n, cot in enumerate((cot_a, cot_b)):
                cot[0] = upper[n]
                cot[ROWS + 1] = lower[n]


def border(first, second, cot_a, cot_b):
    vmem = pl.BlockSpec(memory_space=pltpu.VMEM)
    return pl.pallas_call(
        border_kernel,
        in_specs=[vmem] * 4,
        out_specs=[vmem] * 2,
        out_shape=[pltpu.VMEM(cot_a.shape, BF)] * 2,
        input_output_aliases={2: 0, 3: 1},
        compiler_params=pltpu.CompilerParams(vmem_limit_bytes=4 * MIB),
    )(*in_vmem(first, second, cot_a, cot_b))


STEP = 4


def half_kernel(frame, *refs):
    refs = list(refs)
    take = lambda n: [refs.pop(0) for _ in range(n)]
    lat, act, slope, ft, taps, w1t, w2t = take(7)
    if frame == 0:
        cot_a, cot_b = take(2)
        gl_h, planes_b, gk, gw = take(4)
        planes_a, spread, gm, gp, gl, sem = take(6)
    else:
        planes_a, cot_b, sumk, sumw, _ = take(5)
        gl_h, keep, send = take(3)
        planes_b, spread, gm, gp, gl, sem, gk, gw = take(8)
    n_px = gm.shape[0]
    base = frame * n_px
    zero = jnp.zeros((8, 128), F32)
    for s in range(spread.shape[0]):
        spread[s, 0:8, :] = zero
        spread[s, 264:272, :] = zero

    def split(cells, planes, row, s):
        spread[s, 8:264, :] = cells.astype(F32)
        for c in range(4):
            planes[row, :, 128 * c : 128 * (c + 1)] = spread[s, pl.ds(7 + c, 128, stride=2), :].astype(BF)

    def split_all(cot, planes):
        def body(r, carry):
            for s in range(2):
                split(cot[2 * r + s], planes, 2 * r + s, s)
            return carry

        lax.fori_loop(0, ROWS // 2 + 1, body, 0)

    if frame == 0:
        split_all(cot_a, planes_a)
    split_all(cot_b, planes_b)

    def back(k, carry):
        y = k * STEP
        total = planes_a[pl.ds(y + 1, STEP), :, 128:384].reshape(STEP * 128, 256).astype(F32)
        for dt, planes in ((1, planes_a), (0, planes_b)):
            for dy in range(3):
                window = planes[pl.ds(y + 2 - dy, STEP)].reshape(STEP * 128, 512)
                total = total + dot(window, taps[3 * dt + dy])
        total = (0.5 * total).reshape(STEP // 2, 2, 128, 256)
        upper = total[:, 0].reshape(STEP * 64, 256)
        lower = total[:, 1].reshape(STEP * 64, 256)
        a, b, c, d = upper[:, :128], upper[:, 128:], lower[:, :128], lower[:, 128:]
        ab, am, cd, cm = a + b, a - b, c + d, c - d
        grad = jnp.concatenate([ab + cd, ab - cd, am + cm, am - cm], axis=1).astype(BF)
        start = pl.multiple_of(k * STEP * 64, STEP * 64)
        here = pl.ds(start, STEP * 64)
        gm[here] = grad
        hidden = (dot(grad, w2t[...]) * slope[pl.ds(base + start, STEP * 64)].astype(F32)).astype(BF)
        gp[here] = hidden
        gl[here] = (grad.astype(F32) + dot(hidden, w1t[...])).astype(BF)
        return carry

    lax.fori_loop(0, ROWS // STEP, back, 0)
    out = pltpu.make_async_copy(gl, gl_h.at[pl.ds(base, n_px)], sem)
    out.start()
    for dt, planes in ((1, planes_a), (0, planes_b)):
        cols = planes.reshape((ROWS + 2) * 128, 512)
        for dy in range(3):
            got = dot(ft[frame], cols[128 * (2 - dy) : 128 * (ROWS + 2 - dy)])
            for dx in range(3):
                col = 2 - dx
                both = got[0:128, 128 * col : 128 * (col + 1)] + got[128:256, 128 * (col + 1) : 128 * (col + 2)]
                where = slice(128 * (9 * dt + 3 * dy + dx), 128 * (9 * dt + 3 * dy + dx + 1))
                gk[where] = both if frame == 0 else sumk[where] + both
    for n, (left, right) in enumerate(((lat, gp), (act, gm))):
        for m in range(2):
            part = lax.dot_general(
                left[pl.ds(base, n_px), 256 * m : 256 * (m + 1)],
                right[...],
                (((0,), (0,)), ((), ())),
                preferred_element_type=F32,
            )
            where = slice(512 * n + 256 * m, 512 * n + 256 * (m + 1))
            gw[where] = part if frame == 0 else sumw[where] + part
    if frame == 1:
        ids = block_ids()
        for r in range(8):
            packed = (keep, send)[r // 4].at[r % 4]
            b = ids[r]
            for lane in range(4):
                packed[128 * lane : 128 * (lane + 1), :] = gw[
                    pl.ds(pl.multiple_of(b * 128, 128), 128), 128 * lane : 128 * (lane + 1)
                ].astype(BF)
            packed[512:800, :] = gk[pl.ds(pl.multiple_of(b * 288, 32), 288), :].astype(BF)
    out.wait()


def half(frame, rest, cells, sums=()):
    n = rest[0].shape[0]
    n_px = n // 2
    vmem = pl.BlockSpec(memory_space=pltpu.VMEM)
    any_ = pl.BlockSpec(memory_space=pl.ANY)
    ops = in_vmem(*rest, *cells)
    specs = [vmem] * len(ops)
    planes = (ROWS + 2, 128, 512)
    sum_shapes = [(2304, 128), (1024, 512)]
    scratch = [pltpu.VMEM(planes, BF), pltpu.VMEM((2, 272, 128), F32)]
    scratch += [pltpu.VMEM((n_px, 512), BF)] * 3 + [pltpu.SemaphoreType.DMA]
    shapes = [pltpu.HBM((n, 512), BF)]
    alias = {}
    if frame == 0:
        shapes += [pltpu.VMEM(planes, BF)] + [pltpu.VMEM(shape, F32) for shape in sum_shapes]
    else:
        grad, gk, gw = sums
        alias = {len(ops) + 2: 0}
        ops += in_vmem(gk, gw) + in_hbm(grad)
        specs += [vmem, vmem, any_]
        shapes += [pltpu.VMEM((4, 800, 128), BF)] * 2
        scratch += [pltpu.VMEM(shape, F32) for shape in sum_shapes]
    return pl.pallas_call(
        functools.partial(half_kernel, frame),
        in_specs=specs,
        out_specs=[any_] + [vmem] * (len(shapes) - 1),
        out_shape=shapes,
        input_output_aliases=alias,
        scratch_shapes=scratch,
        cost_estimate=pl.CostEstimate(flops=10 << 30, bytes_accessed=16 * MIB, transcendentals=0),
        compiler_params=pltpu.CompilerParams(vmem_limit_bytes=24 * MIB),
    )(*ops)


def unpack_kernel(own, near, far, last, other, first_h, second_h, gk_h, gw, gk, sems):
    copies = []
    ids = block_ids()
    for r in range(8):
        b = ids[r]
        piece = (own, near, far, last)[r] if r < 4 else other.at[r - 4]
        wide = pl.ds(pl.multiple_of(b * 128, 128), 128)
        low = pl.ds(pl.multiple_of(b * 288, 32), 288)
        for lane in range(4):
            cols = slice(128 * lane, 128 * (lane + 1))
            gw[wide, cols] = piece[cols, :].astype(F32)
        gk[low, :] = piece[512:800, :].astype(F32)
        copies.append(pltpu.make_async_copy(gk.at[low], gk_h.at[low], sems.at[0, r]))
        copies[-1].start()
        down = pl.ds(pl.multiple_of((b % 4) * 128, 128), 128)
        to_first = pltpu.make_async_copy(gw.at[wide], first_h.at[down], sems.at[1, r])
        to_second = pltpu.make_async_copy(gw.at[wide], second_h.at[down], sems.at[1, r])
        pl.when(b < 4)(to_first.start)
        pl.when(b >= 4)(to_second.start)
        copies.append(to_first)
    for copy in copies:
        copy.wait()


def unpack(*pieces):
    vmem = pl.BlockSpec(memory_space=pltpu.VMEM)
    sds = jax.ShapeDtypeStruct
    return pl.pallas_call(
        unpack_kernel,
        in_specs=[vmem] * 5,
        out_specs=[pl.BlockSpec(memory_space=pl.ANY)] * 3,
        out_shape=[sds((512, 512), F32), sds((512, 512), F32), sds((2304, 128), F32)],
        scratch_shapes=[
            pltpu.VMEM((1024, 512), F32),
            pltpu.VMEM((2304, 128), F32),
            pltpu.SemaphoreType.DMA((2, 8)),
        ],
        compiler_params=pltpu.CompilerParams(vmem_limit_bytes=16 << 20),
    )(*pieces)


BOTH = ("ha", "ta")


def coords(device):
    ha, ta = divmod(device, 16)
    return [(ta // 2 % 2) * 2 + ha % 2, ha // 2, ta // 4, ta % 2]


def device_at(x, y, z, core):
    return (y * 2 + x % 2) * 16 + z * 4 + (x // 2) * 2 + core


def along(axes, move):
    pairs = []
    for device in range(128):
        place = coords(device)
        axis = axes[place[3]]
        place[axis] = move(place[axis])
        pairs.append((device, device_at(*place)))
    return pairs


def step_by(count):
    return lambda place: (place + count) % 4


def rounded(value):
    return lax.reduce_precision(value, 8, 7).astype(BF)


def swap(value):
    return lax.ppermute(value, BOTH, [(i, i ^ 1) for i in range(128)])


def trade(near, far, last, axes):
    across = lax.ppermute(far, BOTH, along(axes, step_by(2)))
    before = lax.ppermute(near, BOTH, along(axes, step_by(1)))
    after = lax.ppermute(last, BOTH, along(axes, step_by(3)))
    return before, across, after


def add4(own, before, across, after):
    return rounded((own.astype(F32) + across.astype(F32)) + (before.astype(F32) + after.astype(F32)))


def place():
    ha, ta = lax.axis_index("ha"), lax.axis_index("ta")
    return (ta // 2 % 2) * 2 + ha % 2, ha // 2, ta // 4, ta % 2


def block_ids():
    x, y, _, core = place()
    ids = []
    for other in range(2):
        owner = core ^ other
        start = jnp.where(owner == 0, x, y)
        ids += [owner * 4 + (start + k) % 4 for k in range(4)]
    return ids


def add2(a, b):
    return rounded(a.astype(F32) + b.astype(F32))


def sum_all(keep, send):
    got = swap(send)
    parts = [add2(keep[k], got[k]) for k in range(4)]
    own = add4(parts[0], *trade(*parts[1:], (0, 1)))
    own = add4(own, *trade(own, own, own, (1, 2)))
    own = add4(own, *trade(own, own, own, (2, 0)))
    before, across, after = trade(own, own, own, (0, 1))
    other = swap(jnp.stack([own, after, across, before]))
    return own, after, across, before, other


def neighbour(value, axis, step):
    count = lax.axis_size(axis)
    return lax.ppermute(value, axis, [(i, i + step) for i in range(count) if 0 <= i + step < count])


def meetings(count):
    inner = [(i, i ^ 1) for i in range(count)]
    outer = [(i, i + 1 if i % 2 else i - 1) for i in range(1, count - 1)]
    return inner, outer


def shards(latent, w_first, w_second, kernel, cotangent):
    width = latent.shape[-1]
    flat = latent.reshape(-1, width)
    odd = lax.axis_index("ha") % 2
    top, bottom = cotangent[:, 0], cotangent[:, -1]
    meet = meetings(lax.axis_size("ha"))
    inner = lax.ppermute(jnp.where(odd == 1, top, bottom), "ha", meet[0])
    outer = lax.ppermute(jnp.where(odd == 1, bottom, top), "ha", meet[1])
    *rest, cot_a, cot_b = forward(flat, w_first, w_second, kernel, cotangent)
    cot_a, cot_b = border(inner, outer, cot_a, cot_b)
    later = neighbour(cot_a, "ta", -1)
    grad, planes, gk, gw = half(0, rest, (cot_a, cot_b))
    grad, keep, send = half(1, rest, (planes, later), (grad, gk, gw))
    first, second, gk = unpack(*sum_all(keep, send))
    return grad.reshape(latent.shape), first, second, gk.reshape(kernel.shape)


def solution(mesh):
    return jax.shard_map(
        shards,
        mesh=mesh,
        in_specs=(P("ta", "ha", None, None), P(), P(), P(), P("ta", "ha", None, None)),
        out_specs=(P("ta", "ha", None, None), P(), P(), P()),
        check_vma=False,
    )
```

```python
import functools
import jax
import jax.numpy as jnp
from jax import lax
from jax.experimental import pallas as pl
from jax.experimental.pallas import tpu as pltpu
from jax.sharding import PartitionSpec as P

BF, F32 = jnp.bfloat16, jnp.float32
ROWS = 16
MIB = 1 << 20


def in_hbm(*arrays):
    return [pltpu.with_memory_space_constraint(array, pltpu.HBM) for array in arrays]


def in_vmem(*arrays):
    return [pltpu.with_memory_space_constraint(array, pltpu.VMEM) for array in arrays]


def dot(a, b):
    return jnp.dot(a, b, preferred_element_type=F32)


CHUNK = 1024


def forward_kernel(lat_h, w1_h, w2_h, k_h, cot_h, *refs):
    lat, act, slope, ft, taps, w1t, w2t, cot_a, cot_b, w1, w2, ker, sems = refs
    chunks = lat.shape[0] // CHUNK
    weights = [
        pltpu.make_async_copy(src, dst, sems.at[n])
        for n, (src, dst) in enumerate(((w1_h, w1), (w2_h, w2), (k_h, ker)))
    ]
    frames = [
        pltpu.make_async_copy(cot_h.at[n], dst.at[pl.ds(1, ROWS)], sems.at[3 + n])
        for n, dst in enumerate((cot_a, cot_b))
    ]

    def pixels(k):
        where = pl.ds(k * CHUNK, CHUNK)
        return pltpu.make_async_copy(lat_h.at[where], lat.at[where], sems.at[5 + k])

    weights[0].start()
    pixels(0).start()
    weights[1].start()
    for k in range(1, chunks):
        pixels(k).start()
    weights[2].start()
    for copy in frames:
        copy.start()
    weights[0].wait()
    pixels(0).wait()
    weights[1].wait()

    for k in range(chunks):
        if k:
            pixels(k).wait()
        here = slice(k * CHUNK, (k + 1) * CHUNK)
        x = lat[here]
        pre = dot(x, w1[...])
        sig = 0.5 * jnp.tanh(0.5 * pre) + 0.5
        hidden = pre * sig
        slope[here] = (sig + hidden * (1.0 - sig)).astype(BF)
        hidden = hidden.astype(BF)
        act[here] = hidden
        mixed = 0.5 * (x.astype(F32) + dot(hidden, w2[...]))
        ll, lh, hl, hh = (mixed[:, 128 * b : 128 * (b + 1)] for b in range(4))
        s, d, t, u = ll + lh, ll - lh, hl + hh, hl - hh
        for i in range(CHUNK // 128):
            px = slice(128 * i, 128 * (i + 1))
            for p, (m, n) in enumerate(((s, t), (d, u))):
                row = 2 * (k * CHUNK // 128 + i) + p
                frame, row = row // ROWS, row % ROWS
                lanes = slice(128 * row, 128 * (row + 1))
                ft[frame, 0:128, lanes] = (m[px] + n[px]).astype(BF).T
                ft[frame, 128:256, lanes] = (m[px] - n[px]).astype(BF).T
    w1t[...] = w1[...].T
    w2t[...] = w2[...].T
    weights[2].wait()
    for t in range(6):
        for q in range(2):
            col = 3 * (1 - q)
            taps[t, 128 * col : 128 * (col + 1), 128 * q : 128 * (q + 1)] = jnp.zeros((128, 128), BF)
        for dx in range(3):
            tap = ker[3 * t + dx].T
            for q in range(2):
                col = 2 - dx + q
                taps[t, 128 * col : 128 * (col + 1), 128 * q : 128 * (q + 1)] = tap
    for copy in frames:
        copy.wait()


def forward(latent, w1, w2, kernel, cotangent):
    n = latent.shape[0]
    frame = (ROWS + 2,) + cotangent.shape[2:]
    vmem = pl.BlockSpec(memory_space=pltpu.VMEM)
    shapes = [(n, 512), (n, 512), (n, 512), (2, 256, n), (6, 512, 256), (512, 512), (512, 512), frame, frame]
    return pl.pallas_call(
        forward_kernel,
        in_specs=[pl.BlockSpec(memory_space=pl.ANY)] * 5,
        out_specs=[vmem] * len(shapes),
        out_shape=[pltpu.VMEM(shape, BF) for shape in shapes],
        scratch_shapes=[
            pltpu.VMEM((512, 512), BF),
            pltpu.VMEM((512, 512), BF),
            pltpu.VMEM((18, 128, 128), BF),
            pltpu.SemaphoreType.DMA((5 + n // CHUNK,)),
        ],
        cost_estimate=pl.CostEstimate(flops=8 * n * 512 * 512, bytes_accessed=12 * MIB, transcendentals=n * 512),
        compiler_params=pltpu.CompilerParams(vmem_limit_bytes=16 * MIB),
    )(*in_hbm(latent, w1, w2, kernel.reshape(18, 128, 128), cotangent))


def border_kernel(first, second, _, __, cot_a, cot_b):
    odd = lax.axis_index("ha") % 2
    for upper, lower, here in ((second, first, odd == 0), (first, second, odd == 1)):

        @pl.when(here)
        def _():
            for n, cot in enumerate((cot_a, cot_b)):
                cot[0] = upper[n]
                cot[ROWS + 1] = lower[n]


def border(first, second, cot_a, cot_b):
    vmem = pl.BlockSpec(memory_space=pltpu.VMEM)
    return pl.pallas_call(
        border_kernel,
        in_specs=[vmem] * 4,
        out_specs=[vmem] * 2,
        out_shape=[pltpu.VMEM(cot_a.shape, BF)] * 2,
        input_output_aliases={2: 0, 3: 1},
        compiler_params=pltpu.CompilerParams(vmem_limit_bytes=4 * MIB),
    )(*in_vmem(first, second, cot_a, cot_b))


STEP = 8


def split(cells, planes, spread, row, s):
    spread[s, 8:264, :] = cells[row].astype(F32)
    for c in range(4):
        planes[row, :, 128 * c : 128 * (c + 1)] = spread[s, pl.ds(7 + c, 128, stride=2), :].astype(BF)


def split_all(cells, planes, spread):
    zero = jnp.zeros((8, 128), F32)
    for s in range(2):
        spread[s, 0:8, :] = zero
        spread[s, 264:272, :] = zero

    def body(r, carry):
        for s in range(2):
            split(cells, planes, spread, 2 * r + s, s)
        return carry

    lax.fori_loop(0, ROWS // 2 + 1, body, 0)


def conv(taps, dt, planes, y):
    total = 0.0
    for dy in range(3):
        window = planes[pl.ds(y + 2 - dy, STEP)].reshape(STEP * 128, 512)
        total = total + dot(window, taps[3 * dt + dy])
    return total


def own_cells(planes, y):
    return planes[pl.ds(y + 1, STEP), :, 128:384].reshape(STEP * 128, 256).astype(F32)


def analyze(total):
    total = (0.5 * total).reshape(STEP // 2, 2, 128, 256)
    upper = total[:, 0].reshape(STEP * 64, 256)
    lower = total[:, 1].reshape(STEP * 64, 256)
    a, b, c, d = upper[:, :128], upper[:, 128:], lower[:, :128], lower[:, 128:]
    ab, am, cd, cm = a + b, a - b, c + d, c - d
    return jnp.concatenate([ab + cd, ab - cd, am + cm, am - cm], axis=1).astype(BF)


def rows_of(k, count):
    return pl.ds(pl.multiple_of(k * count, count), count)


def add_taps(gk, ft, dt, planes, before):
    cols = planes.reshape((ROWS + 2) * 128, 512)
    for dy in range(3):
        got = dot(ft, cols[128 * (2 - dy) : 128 * (ROWS + 2 - dy)])
        for dx in range(3):
            col = 2 - dx
            both = got[0:128, 128 * col : 128 * (col + 1)] + got[128:256, 128 * (col + 1) : 128 * (col + 2)]
            where = slice(128 * (9 * dt + 3 * dy + dx), 128 * (9 * dt + 3 * dy + dx + 1))
            gk[where] = both if before is None else before[where] + both


def add_weights(gw, pairs, before):
    for n, (left, right) in enumerate(pairs):
        for m in range(2):
            part = lax.dot_general(
                left[:, 256 * m : 256 * (m + 1)], right[...], (((0,), (0,)), ((), ())), preferred_element_type=F32
            )
            where = slice(512 * n + 256 * m, 512 * n + 256 * (m + 1))
            gw[where] = part if before is None else before[where] + part


def early_kernel(lat, act, slope, ft, taps, w1t, w2t, cot_a, cot_b, gl_h, part, gk, gw, *scratch):
    planes_a, planes_b, spread, gm, gp, gl, sem = scratch
    n_px = gm.shape[0]
    mine = pl.ds(0, n_px)
    split_all(cot_a, planes_a, spread)
    split_all(cot_b, planes_b, spread)

    def back(k, carry):
        y = k * STEP
        total = own_cells(planes_a, y) + conv(taps, 1, planes_a, y) + conv(taps, 0, planes_b, y)
        gm[rows_of(k, STEP * 64)] = analyze(total)
        return carry

    def ahead(k, carry):
        y = k * STEP
        part[rows_of(k, STEP * 128)] = own_cells(planes_b, y) + conv(taps, 1, planes_b, y)
        return carry

    lax.fori_loop(0, ROWS // STEP, back, 0)
    lax.fori_loop(0, ROWS // STEP, ahead, 0)
    gp[...] = (dot(gm[...], w2t[...]) * slope[mine].astype(F32)).astype(BF)
    gl[...] = (gm[...].astype(F32) + dot(gp[...], w1t[...])).astype(BF)
    out = pltpu.make_async_copy(gl, gl_h.at[mine], sem)
    out.start()
    add_taps(gk, ft[0], 1, planes_a, None)
    add_taps(gk, ft[0], 0, planes_b, None)
    add_taps(gk, ft[1], 1, planes_b, gk)
    add_weights(gw, ((lat.at[mine], gp), (act.at[mine], gm)), None)
    out.wait()


def late_kernel(lat, act, slope, ft, taps, w2t, cells, part, sumk, sumw, gm, gp, keep, send, *scratch):
    planes, spread, gk, gw = scratch
    n_px = gm.shape[0]
    mine = pl.ds(n_px, n_px)
    split_all(cells, planes, spread)

    def back(k, carry):
        total = part[rows_of(k, STEP * 128)] + conv(taps, 0, planes, k * STEP)
        gm[rows_of(k, STEP * 64)] = analyze(total)
        return carry

    lax.fori_loop(0, ROWS // STEP, back, 0)
    gp[...] = (dot(gm[...], w2t[...]) * slope[mine].astype(F32)).astype(BF)
    gk[128 * 9 :] = sumk[128 * 9 :]
    add_taps(gk, ft[1], 0, planes, sumk)
    add_weights(gw, ((lat.at[mine], gp), (act.at[mine], gm)), sumw)
    ids = block_ids()
    for r in range(8):
        packed = (keep, send)[r // 4].at[r % 4]
        b = ids[r]
        for lane in range(4):
            packed[128 * lane : 128 * (lane + 1), :] = gw[
                pl.ds(pl.multiple_of(b * 128, 128), 128), 128 * lane : 128 * (lane + 1)
            ].astype(BF)
        packed[512:800, :] = gk[pl.ds(pl.multiple_of(b * 288, 32), 288), :].astype(BF)


def last_kernel(gm, gp, w1t, _, gl_h, gl, sem):
    n_px = gm.shape[0]
    gl[...] = (gm[...].astype(F32) + dot(gp[...], w1t[...])).astype(BF)
    out = pltpu.make_async_copy(gl, gl_h.at[pl.ds(n_px, n_px)], sem)
    out.start()
    out.wait()


VMEM_SPEC = pl.BlockSpec(memory_space=pltpu.VMEM)
ANY_SPEC = pl.BlockSpec(memory_space=pl.ANY)
PLANES = (ROWS + 2, 128, 512)
SUMS = [(2304, 128), (1024, 512)]
SPREAD = (2, 272, 128)


def early(lat, act, slope, ft, taps, w1t, w2t, cot_a, cot_b):
    n_px = lat.shape[0] // 2
    sums = [pltpu.VMEM(shape, F32) for shape in SUMS]
    ops = in_vmem(lat, act, slope, ft, taps, w1t, w2t, cot_a, cot_b)
    return pl.pallas_call(
        early_kernel,
        in_specs=[VMEM_SPEC] * len(ops),
        out_specs=[ANY_SPEC] + [VMEM_SPEC] * 3,
        out_shape=[pltpu.HBM(lat.shape, BF), pltpu.VMEM((ROWS * 128, 256), F32)] + sums,
        scratch_shapes=[pltpu.VMEM(PLANES, BF)] * 2
        + [pltpu.VMEM(SPREAD, F32)]
        + [pltpu.VMEM((n_px, 512), BF)] * 3
        + [pltpu.SemaphoreType.DMA],
        cost_estimate=pl.CostEstimate(flops=10 << 30, bytes_accessed=16 * MIB, transcendentals=0),
        compiler_params=pltpu.CompilerParams(vmem_limit_bytes=24 * MIB),
    )(*ops)


def late(lat, act, slope, ft, taps, w2t, cells, part, gk, gw):
    half = (lat.shape[0] // 2, 512)
    ops = in_vmem(lat, act, slope, ft, taps, w2t, cells, part, gk, gw)
    return pl.pallas_call(
        late_kernel,
        in_specs=[VMEM_SPEC] * len(ops),
        out_specs=[VMEM_SPEC] * 4,
        out_shape=[pltpu.VMEM(half, BF)] * 2 + [pltpu.VMEM((4, 800, 128), BF)] * 2,
        scratch_shapes=[pltpu.VMEM(PLANES, BF), pltpu.VMEM(SPREAD, F32)]
        + [pltpu.VMEM(shape, F32) for shape in SUMS],
        cost_estimate=pl.CostEstimate(flops=6 << 30, bytes_accessed=16 * MIB, transcendentals=0),
        compiler_params=pltpu.CompilerParams(vmem_limit_bytes=24 * MIB),
    )(*ops)


def last(gm, gp, w1t, grad):
    return pl.pallas_call(
        last_kernel,
        in_specs=[VMEM_SPEC] * 3 + [ANY_SPEC],
        out_specs=ANY_SPEC,
        out_shape=pltpu.HBM(grad.shape, BF),
        input_output_aliases={3: 0},
        scratch_shapes=[pltpu.VMEM(gm.shape, BF), pltpu.SemaphoreType.DMA],
        cost_estimate=pl.CostEstimate(flops=1 << 29, bytes_accessed=4 * MIB, transcendentals=0),
        compiler_params=pltpu.CompilerParams(vmem_limit_bytes=8 * MIB),
    )(*in_vmem(gm, gp, w1t), *in_hbm(grad))


def unpack_kernel(own, near, far, last, other, first_h, second_h, gk_h, gw, gk, sems):
    copies = []
    ids = block_ids()
    for r in range(8):
        b = ids[r]
        piece = (own, near, far, last)[r] if r < 4 else other.at[r - 4]
        wide = pl.ds(pl.multiple_of(b * 128, 128), 128)
        low = pl.ds(pl.multiple_of(b * 288, 32), 288)
        for lane in range(4):
            cols = slice(128 * lane, 128 * (lane + 1))
            gw[wide, cols] = piece[cols, :].astype(F32)
        gk[low, :] = piece[512:800, :].astype(F32)
        copies.append(pltpu.make_async_copy(gk.at[low], gk_h.at[low], sems.at[0, r]))
        copies[-1].start()
        down = pl.ds(pl.multiple_of((b % 4) * 128, 128), 128)
        to_first = pltpu.make_async_copy(gw.at[wide], first_h.at[down], sems.at[1, r])
        to_second = pltpu.make_async_copy(gw.at[wide], second_h.at[down], sems.at[1, r])
        pl.when(b < 4)(to_first.start)
        pl.when(b >= 4)(to_second.start)
        copies.append(to_first)
    for copy in copies:
        copy.wait()


def unpack(*pieces):
    vmem = pl.BlockSpec(memory_space=pltpu.VMEM)
    sds = jax.ShapeDtypeStruct
    return pl.pallas_call(
        unpack_kernel,
        in_specs=[vmem] * 5,
        out_specs=[pl.BlockSpec(memory_space=pl.ANY)] * 3,
        out_shape=[sds((512, 512), F32), sds((512, 512), F32), sds((2304, 128), F32)],
        scratch_shapes=[
            pltpu.VMEM((1024, 512), F32),
            pltpu.VMEM((2304, 128), F32),
            pltpu.SemaphoreType.DMA((2, 8)),
        ],
        compiler_params=pltpu.CompilerParams(vmem_limit_bytes=16 << 20),
    )(*pieces)


BOTH = ("ha", "ta")


def coords(device):
    ha, ta = divmod(device, 16)
    return [(ta // 2 % 2) * 2 + ha % 2, ha // 2, ta // 4, ta % 2]


def device_at(x, y, z, core):
    return (y * 2 + x % 2) * 16 + z * 4 + (x // 2) * 2 + core


def along(axes, move):
    pairs = []
    for device in range(128):
        place = coords(device)
        axis = axes[place[3]]
        place[axis] = move(place[axis])
        pairs.append((device, device_at(*place)))
    return pairs


def step_by(count):
    return lambda place: (place + count) % 4


def rounded(value):
    return lax.reduce_precision(value, 8, 7).astype(BF)


def swap(value):
    return lax.ppermute(value, BOTH, [(i, i ^ 1) for i in range(128)])


def trade(near, far, last, axes):
    across = lax.ppermute(far, BOTH, along(axes, step_by(2)))
    before = lax.ppermute(near, BOTH, along(axes, step_by(1)))
    after = lax.ppermute(last, BOTH, along(axes, step_by(3)))
    return before, across, after


def add4(own, before, across, after):
    return rounded((own.astype(F32) + across.astype(F32)) + (before.astype(F32) + after.astype(F32)))


def place():
    ha, ta = lax.axis_index("ha"), lax.axis_index("ta")
    return (ta // 2 % 2) * 2 + ha % 2, ha // 2, ta // 4, ta % 2


def block_ids():
    x, y, _, core = place()
    ids = []
    for other in range(2):
        owner = core ^ other
        start = jnp.where(owner == 0, x, y)
        ids += [owner * 4 + (start + k) % 4 for k in range(4)]
    return ids


def add2(a, b):
    return rounded(a.astype(F32) + b.astype(F32))


def sum_all(keep, got):
    parts = [add2(keep[k], got[k]) for k in range(4)]
    own = add4(parts[0], *trade(*parts[1:], (0, 1)))
    own = add4(own, *trade(own, own, own, (1, 2)))
    own = add4(own, *trade(own, own, own, (2, 0)))
    before, across, after = trade(own, own, own, (0, 1))
    other = swap(jnp.stack([own, after, across, before]))
    return own, after, across, before, other


def neighbour(value, axis, step):
    count = lax.axis_size(axis)
    return lax.ppermute(value, axis, [(i, i + step) for i in range(count) if 0 <= i + step < count])


def meetings(count):
    inner = [(i, i ^ 1) for i in range(count)]
    outer = [(i, i + 1 if i % 2 else i - 1) for i in range(1, count - 1)]
    return inner, outer


def shards(latent, w_first, w_second, kernel, cotangent):
    width = latent.shape[-1]
    flat = latent.reshape(-1, width)
    odd = lax.axis_index("ha") % 2
    top, bottom = cotangent[:, 0], cotangent[:, -1]
    meet = meetings(lax.axis_size("ha"))
    inner = lax.ppermute(jnp.where(odd == 1, top, bottom), "ha", meet[0])
    outer = lax.ppermute(jnp.where(odd == 1, bottom, top), "ha", meet[1])
    *rest, cot_a, cot_b = forward(flat, w_first, w_second, kernel, cotangent)
    cot_a, cot_b = border(inner, outer, cot_a, cot_b)
    later = neighbour(cot_a, "ta", -1)
    lat, act, slope, ft, taps, w1t, w2t = rest
    grad, part, gk, gw = early(*rest, cot_a, cot_b)
    gm, gp, keep, send = late(lat, act, slope, ft, taps, w2t, later, part, gk, gw)
    got = swap(send)
    grad = last(gm, gp, w1t, grad)
    got, grad = lax.optimization_barrier((got, grad))
    first, second, gk = unpack(*sum_all(keep, got))
    return grad.reshape(latent.shape), first, second, gk.reshape(kernel.shape)


def solution(mesh):
    return jax.shard_map(
        shards,
        mesh=mesh,
        in_specs=(P("ta", "ha", None, None), P(), P(), P(), P("ta", "ha", None, None)),
        out_specs=(P("ta", "ha", None, None), P(), P(), P()),
        check_vma=False,
    )
```

```python
import functools
import jax
import jax.numpy as jnp
from jax import lax
from jax.experimental import pallas as pl
from jax.experimental.pallas import tpu as pltpu
from jax.sharding import PartitionSpec as P

BF, F32 = jnp.bfloat16, jnp.float32
ROWS = 16
MIB = 1 << 20


def in_hbm(*arrays):
    return [pltpu.with_memory_space_constraint(array, pltpu.HBM) for array in arrays]


def in_vmem(*arrays):
    return [pltpu.with_memory_space_constraint(array, pltpu.VMEM) for array in arrays]


def dot(a, b):
    return jnp.dot(a, b, preferred_element_type=F32)


def project(x, w1, w2, act, slope, ft):
    pre = dot(x, w1[...])
    sig = 0.5 * jnp.tanh(0.5 * pre) + 0.5
    hidden = pre * sig
    slope[...] = (sig + hidden * (1.0 - sig)).astype(BF)
    hidden = hidden.astype(BF)
    act[...] = hidden
    mixed = 0.5 * (x.astype(F32) + dot(hidden, w2[...]))
    ll, lh, hl, hh = (mixed[:, 128 * b : 128 * (b + 1)] for b in range(4))
    s, d, t, u = ll + lh, ll - lh, hl + hh, hl - hh
    for i in range(x.shape[0] // 128):
        px = slice(128 * i, 128 * (i + 1))
        for p, (m, n) in enumerate(((s, t), (d, u))):
            row = 2 * i + p
            lanes = slice(128 * row, 128 * (row + 1))
            ft[0:128, lanes] = (m[px] + n[px]).astype(BF).T
            ft[128:256, lanes] = (m[px] - n[px]).astype(BF).T


def first_kernel(lat_h, w1_h, w2_h, k_h, cot_h, lat, w1, w2, ker, cot_a, cot_b, act, slope, ft, sems):
    n_px = act.shape[0]
    pairs = [(w1_h, w1), (lat_h.at[pl.ds(0, n_px)], lat.at[pl.ds(0, n_px)]), (w2_h, w2)]
    pairs += [(cot_h.at[n], dst.at[pl.ds(1, ROWS)]) for n, dst in enumerate((cot_a, cot_b))]
    pairs += [(lat_h.at[pl.ds(n_px, n_px)], lat.at[pl.ds(n_px, n_px)]), (k_h, ker)]
    copies = [pltpu.make_async_copy(src, dst, sems.at[n]) for n, (src, dst) in enumerate(pairs)]
    for copy in copies:
        copy.start()
    for copy in copies[:3]:
        copy.wait()
    project(lat[0:n_px], w1, w2, act, slope, ft)
    for copy in copies[3:]:
        copy.wait()


def second_kernel(lat, w1, w2, ker, _, act, slope, ft, taps, w1t, w2t):
    n_px = act.shape[0]
    project(lat[n_px : 2 * n_px], w1, w2, act, slope, ft)
    w1t[...] = w1[...].T
    w2t[...] = w2[...].T
    for t in range(6):
        for q in range(2):
            col = 3 * (1 - q)
            taps[t, 128 * col : 128 * (col + 1), 128 * q : 128 * (q + 1)] = jnp.zeros((128, 128), BF)
        for dx in range(3):
            tap = ker[3 * t + dx].T
            for q in range(2):
                col = 2 - dx + q
                taps[t, 128 * col : 128 * (col + 1), 128 * q : 128 * (q + 1)] = tap


VMEM_SPEC = pl.BlockSpec(memory_space=pltpu.VMEM)
ANY_SPEC = pl.BlockSpec(memory_space=pl.ANY)


def frame_shapes(n_px):
    return [(n_px, 512), (n_px, 512), (256, 2 * n_px)]


def first(latent, w1, w2, kernel, cotangent):
    n = latent.shape[0]
    frame = (ROWS + 2,) + cotangent.shape[2:]
    shapes = [(n, 512), (512, 512), (512, 512), (18, 128, 128), frame, frame] + frame_shapes(n // 2)
    return pl.pallas_call(
        first_kernel,
        in_specs=[ANY_SPEC] * 5,
        out_specs=[VMEM_SPEC] * len(shapes),
        out_shape=[pltpu.VMEM(shape, BF) for shape in shapes],
        scratch_shapes=[pltpu.SemaphoreType.DMA((7,))],
        cost_estimate=pl.CostEstimate(flops=4 * n * 512 * 512, bytes_accessed=8 * MIB, transcendentals=n * 256),
        compiler_params=pltpu.CompilerParams(vmem_limit_bytes=16 * MIB),
    )(*in_hbm(latent, w1, w2, kernel.reshape(18, 128, 128), cotangent))


def second(lat, w1, w2, ker, after):
    n = lat.shape[0]
    shapes = frame_shapes(n // 2) + [(6, 512, 256), (512, 512), (512, 512)]
    return pl.pallas_call(
        second_kernel,
        in_specs=[VMEM_SPEC] * 4 + [ANY_SPEC],
        out_specs=[VMEM_SPEC] * len(shapes),
        out_shape=[pltpu.VMEM(shape, BF) for shape in shapes],
        cost_estimate=pl.CostEstimate(flops=4 * n * 512 * 512, bytes_accessed=8 * MIB, transcendentals=n * 256),
        compiler_params=pltpu.CompilerParams(vmem_limit_bytes=16 * MIB),
    )(*in_vmem(lat, w1, w2, ker, after))


def border_kernel(first, second, _, __, cot_a, cot_b):
    odd = lax.axis_index("ha") % 2
    for upper, lower, here in ((second, first, odd == 0), (first, second, odd == 1)):

        @pl.when(here)
        def _():
            for n, cot in enumerate((cot_a, cot_b)):
                cot[0] = upper[n]
                cot[ROWS + 1] = lower[n]


def border(first, second, cot_a, cot_b):
    vmem = pl.BlockSpec(memory_space=pltpu.VMEM)
    return pl.pallas_call(
        border_kernel,
        in_specs=[vmem] * 4,
        out_specs=[vmem] * 2,
        out_shape=[pltpu.VMEM(cot_a.shape, BF)] * 2,
        input_output_aliases={2: 0, 3: 1},
        compiler_params=pltpu.CompilerParams(vmem_limit_bytes=4 * MIB),
    )(*in_vmem(first, second, cot_a, cot_b))


STEP = 8


def split(cells, planes, spread, row, s):
    spread[s, 8:264, :] = cells[row].astype(F32)
    for c in range(4):
        planes[row, :, 128 * c : 128 * (c + 1)] = spread[s, pl.ds(7 + c, 128, stride=2), :].astype(BF)


def split_all(cells, planes, spread):
    zero = jnp.zeros((8, 128), F32)
    for s in range(2):
        spread[s, 0:8, :] = zero
        spread[s, 264:272, :] = zero

    def body(r, carry):
        for s in range(2):
            split(cells, planes, spread, 2 * r + s, s)
        return carry

    lax.fori_loop(0, ROWS // 2 + 1, body, 0)


def conv(taps, dt, planes, y):
    total = 0.0
    for dy in range(3):
        window = planes[pl.ds(y + 2 - dy, STEP)].reshape(STEP * 128, 512)
        total = total + dot(window, taps[3 * dt + dy])
    return total


def own_cells(planes, y):
    return planes[pl.ds(y + 1, STEP), :, 128:384].reshape(STEP * 128, 256).astype(F32)


def analyze(total):
    total = (0.5 * total).reshape(STEP // 2, 2, 128, 256)
    upper = total[:, 0].reshape(STEP * 64, 256)
    lower = total[:, 1].reshape(STEP * 64, 256)
    a, b, c, d = upper[:, :128], upper[:, 128:], lower[:, :128], lower[:, 128:]
    ab, am, cd, cm = a + b, a - b, c + d, c - d
    return jnp.concatenate([ab + cd, ab - cd, am + cm, am - cm], axis=1).astype(BF)


def rows_of(k, count):
    return pl.ds(pl.multiple_of(k * count, count), count)


def add_taps(gk, ft, dt, planes, before):
    cols = planes.reshape((ROWS + 2) * 128, 512)
    for dy in range(3):
        got = dot(ft[...], cols[128 * (2 - dy) : 128 * (ROWS + 2 - dy)])
        for dx in range(3):
            col = 2 - dx
            both = got[0:128, 128 * col : 128 * (col + 1)] + got[128:256, 128 * (col + 1) : 128 * (col + 2)]
            where = slice(128 * (9 * dt + 3 * dy + dx), 128 * (9 * dt + 3 * dy + dx + 1))
            gk[where] = both if before is None else before[where] + both


def add_weights(gw, pairs, before):
    for n, (left, right) in enumerate(pairs):
        for m in range(2):
            part = lax.dot_general(
                left[:, 256 * m : 256 * (m + 1)], right[...], (((0,), (0,)), ((), ())), preferred_element_type=F32
            )
            where = slice(512 * n + 256 * m, 512 * n + 256 * (m + 1))
            gw[where] = part if before is None else before[where] + part


def early_kernel(lat, act, slope, ft_a, ft_b, taps, w1t, w2t, cot_a, cot_b, gl_h, part, gk, gw, *scratch):
    planes_a, planes_b, spread, gm, gp, gl, sem = scratch
    n_px = gm.shape[0]
    mine = pl.ds(0, n_px)
    split_all(cot_a, planes_a, spread)
    split_all(cot_b, planes_b, spread)

    def back(k, carry):
        y = k * STEP
        total = own_cells(planes_a, y) + conv(taps, 1, planes_a, y) + conv(taps, 0, planes_b, y)
        gm[rows_of(k, STEP * 64)] = analyze(total)
        return carry

    def ahead(k, carry):
        y = k * STEP
        part[rows_of(k, STEP * 128)] = own_cells(planes_b, y) + conv(taps, 1, planes_b, y)
        return carry

    lax.fori_loop(0, ROWS // STEP, back, 0)
    lax.fori_loop(0, ROWS // STEP, ahead, 0)
    gp[...] = (dot(gm[...], w2t[...]) * slope[...].astype(F32)).astype(BF)
    gl[...] = (gm[...].astype(F32) + dot(gp[...], w1t[...])).astype(BF)
    out = pltpu.make_async_copy(gl, gl_h.at[mine], sem)
    out.start()
    add_taps(gk, ft_a, 1, planes_a, None)
    add_taps(gk, ft_a, 0, planes_b, None)
    add_taps(gk, ft_b, 1, planes_b, gk)
    add_weights(gw, ((lat.at[mine], gp), (act, gm)), None)
    out.wait()


def late_kernel(lat, act, slope, ft, taps, w2t, cells, part, sumk, sumw, gm, gp, keep, send, *scratch):
    planes, spread, gk, gw = scratch
    n_px = gm.shape[0]
    mine = pl.ds(n_px, n_px)
    split_all(cells, planes, spread)

    def back(k, carry):
        total = part[rows_of(k, STEP * 128)] + conv(taps, 0, planes, k * STEP)
        gm[rows_of(k, STEP * 64)] = analyze(total)
        return carry

    lax.fori_loop(0, ROWS // STEP, back, 0)
    gp[...] = (dot(gm[...], w2t[...]) * slope[...].astype(F32)).astype(BF)
    gk[128 * 9 :] = sumk[128 * 9 :]
    add_taps(gk, ft, 0, planes, sumk)
    add_weights(gw, ((lat.at[mine], gp), (act, gm)), sumw)
    ids = block_ids()
    for r in range(8):
        packed = (keep, send)[r // 4].at[r % 4]
        b = ids[r]
        for lane in range(4):
            packed[128 * lane : 128 * (lane + 1), :] = gw[
                pl.ds(pl.multiple_of(b * 128, 128), 128), 128 * lane : 128 * (lane + 1)
            ].astype(BF)
        packed[512:800, :] = gk[pl.ds(pl.multiple_of(b * 288, 32), 288), :].astype(BF)


def last_kernel(gm, gp, w1t, _, gl_h, gl, sem):
    n_px = gm.shape[0]
    gl[...] = (gm[...].astype(F32) + dot(gp[...], w1t[...])).astype(BF)
    out = pltpu.make_async_copy(gl, gl_h.at[pl.ds(n_px, n_px)], sem)
    out.start()
    out.wait()


PLANES = (ROWS + 2, 128, 512)
SUMS = [(2304, 128), (1024, 512)]
SPREAD = (2, 272, 128)


def early(lat, *rest):
    n_px = lat.shape[0] // 2
    sums = [pltpu.VMEM(shape, F32) for shape in SUMS]
    ops = in_vmem(lat, *rest)
    return pl.pallas_call(
        early_kernel,
        in_specs=[VMEM_SPEC] * len(ops),
        out_specs=[ANY_SPEC] + [VMEM_SPEC] * 3,
        out_shape=[pltpu.HBM(lat.shape, BF), pltpu.VMEM((ROWS * 128, 256), F32)] + sums,
        scratch_shapes=[pltpu.VMEM(PLANES, BF)] * 2
        + [pltpu.VMEM(SPREAD, F32)]
        + [pltpu.VMEM((n_px, 512), BF)] * 3
        + [pltpu.SemaphoreType.DMA],
        cost_estimate=pl.CostEstimate(flops=10 << 30, bytes_accessed=16 * MIB, transcendentals=0),
        compiler_params=pltpu.CompilerParams(vmem_limit_bytes=24 * MIB),
    )(*ops)


def late(lat, act, slope, ft, taps, w2t, cells, part, gk, gw):
    half = (lat.shape[0] // 2, 512)
    ops = in_vmem(lat, act, slope, ft, taps, w2t, cells, part, gk, gw)
    return pl.pallas_call(
        late_kernel,
        in_specs=[VMEM_SPEC] * len(ops),
        out_specs=[VMEM_SPEC] * 4,
        out_shape=[pltpu.VMEM(half, BF)] * 2 + [pltpu.VMEM((4, 800, 128), BF)] * 2,
        scratch_shapes=[pltpu.VMEM(PLANES, BF), pltpu.VMEM(SPREAD, F32)]
        + [pltpu.VMEM(shape, F32) for shape in SUMS],
        cost_estimate=pl.CostEstimate(flops=6 << 30, bytes_accessed=16 * MIB, transcendentals=0),
        compiler_params=pltpu.CompilerParams(vmem_limit_bytes=24 * MIB),
    )(*ops)


def last(gm, gp, w1t, grad):
    return pl.pallas_call(
        last_kernel,
        in_specs=[VMEM_SPEC] * 3 + [ANY_SPEC],
        out_specs=ANY_SPEC,
        out_shape=pltpu.HBM(grad.shape, BF),
        input_output_aliases={3: 0},
        scratch_shapes=[pltpu.VMEM(gm.shape, BF), pltpu.SemaphoreType.DMA],
        cost_estimate=pl.CostEstimate(flops=1 << 29, bytes_accessed=4 * MIB, transcendentals=0),
        compiler_params=pltpu.CompilerParams(vmem_limit_bytes=8 * MIB),
    )(*in_vmem(gm, gp, w1t), *in_hbm(grad))


def unpack_kernel(side, *refs):
    if side:
        (other, *_), refs = refs[:4], refs[4:]
        pieces = [other.at[r] for r in range(4)]
    else:
        pieces, refs = refs[:4], refs[4:]
    first_h, second_h, gk_h, gw, gk, sems = refs
    copies = []
    ids = block_ids()[4 * side : 4 * side + 4]
    for r in range(4):
        b, piece = ids[r], pieces[r]
        down = pl.ds(pl.multiple_of((b % 4) * 128, 128), 128)
        low = pl.ds(pl.multiple_of(b * 288, 32), 288)
        for lane in range(4):
            cols = slice(128 * lane, 128 * (lane + 1))
            gw[r, :, cols] = piece[cols, :].astype(F32)
        gk[r] = piece[512:800, :].astype(F32)
        copies.append(pltpu.make_async_copy(gk.at[r], gk_h.at[low], sems.at[0, r]))
        copies[-1].start()
        to_first = pltpu.make_async_copy(gw.at[r], first_h.at[down], sems.at[1, r])
        to_second = pltpu.make_async_copy(gw.at[r], second_h.at[down], sems.at[1, r])
        pl.when(b < 4)(to_first.start)
        pl.when(b >= 4)(to_second.start)
        copies.append(to_first)
    for copy in copies:
        copy.wait()


def unpack(side, pieces, outs=()):
    return pl.pallas_call(
        functools.partial(unpack_kernel, side),
        in_specs=[VMEM_SPEC] * len(pieces) + [ANY_SPEC] * len(outs),
        out_specs=[ANY_SPEC] * 3,
        out_shape=[pltpu.HBM(shape, F32) for shape in ((512, 512), (512, 512), (2304, 128))],
        input_output_aliases={1 + n: n for n in range(len(outs))},
        scratch_shapes=[
            pltpu.VMEM((4, 128, 512), F32),
            pltpu.VMEM((4, 288, 128), F32),
            pltpu.SemaphoreType.DMA((2, 4)),
        ],
        cost_estimate=pl.CostEstimate(flops=1 << 20, bytes_accessed=3 * MIB, transcendentals=0),
        compiler_params=pltpu.CompilerParams(vmem_limit_bytes=8 * MIB),
    )(*pieces, *in_hbm(*outs))


BOTH = ("ha", "ta")


def coords(device):
    ha, ta = divmod(device, 16)
    return [(ta // 2 % 2) * 2 + ha % 2, ha // 2, ta // 4, ta % 2]


def device_at(x, y, z, core):
    return (y * 2 + x % 2) * 16 + z * 4 + (x // 2) * 2 + core


def along(axes, move):
    pairs = []
    for device in range(128):
        place = coords(device)
        axis = axes[place[3]]
        place[axis] = move(place[axis])
        pairs.append((device, device_at(*place)))
    return pairs


def step_by(count):
    return lambda place: (place + count) % 4


def rounded(value):
    return lax.reduce_precision(value, 8, 7).astype(BF)


def swap(value):
    return lax.ppermute(value, BOTH, [(i, i ^ 1) for i in range(128)])


def trade(near, far, last, axes):
    across = lax.ppermute(far, BOTH, along(axes, step_by(2)))
    before = lax.ppermute(near, BOTH, along(axes, step_by(1)))
    after = lax.ppermute(last, BOTH, along(axes, step_by(3)))
    return before, across, after


def add4(own, before, across, after):
    return rounded((own.astype(F32) + across.astype(F32)) + (before.astype(F32) + after.astype(F32)))


def place():
    ha, ta = lax.axis_index("ha"), lax.axis_index("ta")
    return (ta // 2 % 2) * 2 + ha % 2, ha // 2, ta // 4, ta % 2


def block_ids():
    _, y, z, core = place()
    ids = []
    for other in range(2):
        owner = core ^ other
        start = jnp.where(owner == 0, z, y)
        ids += [owner * 4 + (start + k) % 4 for k in range(4)]
    return ids


def add2(a, b):
    return rounded(a.astype(F32) + b.astype(F32))


def sum_all(keep, got):
    parts = [add2(keep[k], got[k]) for k in range(4)]
    own = add4(parts[0], *trade(*parts[1:], (2, 1)))
    own = add4(own, *trade(own, own, own, (1, 0)))
    own = add4(own, *trade(own, own, own, (0, 2)))
    before, across, after = trade(own, own, own, (2, 1))
    other = swap(jnp.stack([own, after, across, before]))
    outs = unpack(0, (own, after, across, before))
    return unpack(1, (other,), outs)


def neighbour(value, axis, step):
    count = lax.axis_size(axis)
    return lax.ppermute(value, axis, [(i, i + step) for i in range(count) if 0 <= i + step < count])


def meetings(count):
    inner = [(i, i ^ 1) for i in range(count)]
    outer = [(i, i + 1 if i % 2 else i - 1) for i in range(1, count - 1)]
    return inner, outer


def shards(latent, w_first, w_second, kernel, cotangent):
    width = latent.shape[-1]
    flat = latent.reshape(-1, width)
    odd = lax.axis_index("ha") % 2
    top, bottom = cotangent[:, 0], cotangent[:, -1]
    meet = meetings(lax.axis_size("ha"))
    inner = lax.ppermute(jnp.where(odd == 1, top, bottom), "ha", meet[0])
    outer = lax.ppermute(jnp.where(odd == 1, bottom, top), "ha", meet[1])
    lat, w1, w2, ker, cot_a, cot_b, act_a, slope_a, ft_a = first(flat, w_first, w_second, kernel, cotangent)
    cot_a, cot_b = border(inner, outer, cot_a, cot_b)
    later = neighbour(cot_a, "ta", -1)
    act_b, slope_b, ft_b, taps, w1t, w2t = second(lat, w1, w2, ker, cot_b)
    grad, part, gk, gw = early(lat, act_a, slope_a, ft_a, ft_b, taps, w1t, w2t, cot_a, cot_b)
    gm, gp, keep, send = late(lat, act_b, slope_b, ft_b, taps, w2t, later, part, gk, gw)
    got = swap(send)
    grad = last(gm, gp, w1t, grad)
    got, grad = lax.optimization_barrier((got, grad))
    grad_first, grad_second, gk = sum_all(keep, got)
    return grad.reshape(latent.shape), grad_first, grad_second, gk.reshape(kernel.shape)


def solution(mesh):
    return jax.shard_map(
        shards,
        mesh=mesh,
        in_specs=(P("ta", "ha", None, None), P(), P(), P(), P("ta", "ha", None, None)),
        out_specs=(P("ta", "ha", None, None), P(), P(), P()),
        check_vma=False,
    )
```

```python
import functools
import jax
import jax.numpy as jnp
from jax import lax
from jax.experimental import pallas as pl
from jax.experimental.pallas import tpu as pltpu
from jax.sharding import PartitionSpec as P

BF, F32 = jnp.bfloat16, jnp.float32
ROWS = 16
MIB = 1 << 20


def in_hbm(*arrays):
    return [pltpu.with_memory_space_constraint(array, pltpu.HBM) for array in arrays]


def in_vmem(*arrays):
    return [pltpu.with_memory_space_constraint(array, pltpu.VMEM) for array in arrays]


def dot(a, b):
    return jnp.dot(a, b, preferred_element_type=F32)


def project(x, w1, w2, act, slope, ft):
    pre = dot(x, w1[...])
    sig = 0.5 * jnp.tanh(0.5 * pre) + 0.5
    hidden = pre * sig
    slope[...] = (sig + hidden * (1.0 - sig)).astype(BF)
    hidden = hidden.astype(BF)
    act[...] = hidden
    mixed = 0.5 * (x.astype(F32) + dot(hidden, w2[...]))
    ll, lh, hl, hh = (mixed[:, 128 * b : 128 * (b + 1)] for b in range(4))
    s, d, t, u = ll + lh, ll - lh, hl + hh, hl - hh
    for i in range(x.shape[0] // 128):
        px = slice(128 * i, 128 * (i + 1))
        for p, (m, n) in enumerate(((s, t), (d, u))):
            row = 2 * i + p
            lanes = slice(128 * row, 128 * (row + 1))
            ft[0:128, lanes] = (m[px] + n[px]).astype(BF).T
            ft[128:256, lanes] = (m[px] - n[px]).astype(BF).T


def first_kernel(lat_h, w1_h, w2_h, k_h, cot_h, lat, w1, w2, ker, cot_a, cot_b, act, slope, ft, sems):
    n_px = act.shape[0]
    pairs = [(w1_h, w1), (lat_h.at[pl.ds(0, n_px)], lat.at[pl.ds(0, n_px)]), (w2_h, w2)]
    pairs += [(cot_h.at[n], dst.at[pl.ds(1, ROWS)]) for n, dst in enumerate((cot_a, cot_b))]
    pairs += [(lat_h.at[pl.ds(n_px, n_px)], lat.at[pl.ds(n_px, n_px)]), (k_h, ker)]
    copies = [pltpu.make_async_copy(src, dst, sems.at[n]) for n, (src, dst) in enumerate(pairs)]
    for copy in copies:
        copy.start()
    for copy in copies[:3]:
        copy.wait()
    project(lat[0:n_px], w1, w2, act, slope, ft)
    for copy in copies[3:]:
        copy.wait()


def turn(w1, w2, ker, taps, w1t, w2t):
    w1t[...] = w1[...].T
    w2t[...] = w2[...].T
    for t in range(6):
        for q in range(2):
            col = 3 * (1 - q)
            taps[t, 128 * col : 128 * (col + 1), 128 * q : 128 * (q + 1)] = jnp.zeros((128, 128), BF)
        for dx in range(3):
            tap = ker[3 * t + dx].T
            for q in range(2):
                col = 2 - dx + q
                taps[t, 128 * col : 128 * (col + 1), 128 * q : 128 * (q + 1)] = tap


VMEM_SPEC = pl.BlockSpec(memory_space=pltpu.VMEM)
ANY_SPEC = pl.BlockSpec(memory_space=pl.ANY)


def frame_shapes(n_px):
    return [(n_px, 512), (n_px, 512), (256, 2 * n_px)]


def first(latent, w1, w2, kernel, cotangent):
    n = latent.shape[0]
    frame = (ROWS + 2,) + cotangent.shape[2:]
    shapes = [(n, 512), (512, 512), (512, 512), (18, 128, 128), frame, frame] + frame_shapes(n // 2)
    return pl.pallas_call(
        first_kernel,
        in_specs=[ANY_SPEC] * 5,
        out_specs=[VMEM_SPEC] * len(shapes),
        out_shape=[pltpu.VMEM(shape, BF) for shape in shapes],
        scratch_shapes=[pltpu.SemaphoreType.DMA((7,))],
        cost_estimate=pl.CostEstimate(flops=4 * n * 512 * 512, bytes_accessed=8 * MIB, transcendentals=n * 256),
        compiler_params=pltpu.CompilerParams(vmem_limit_bytes=16 * MIB),
    )(*in_hbm(latent, w1, w2, kernel.reshape(18, 128, 128), cotangent))


def border_kernel(first, second, _, __, cot_a, cot_b):
    odd = lax.axis_index("ha") % 2
    for upper, lower, here in ((second, first, odd == 0), (first, second, odd == 1)):

        @pl.when(here)
        def _():
            for n, cot in enumerate((cot_a, cot_b)):
                cot[0] = upper[n]
                cot[ROWS + 1] = lower[n]


def border(first, second, cot_a, cot_b):
    vmem = pl.BlockSpec(memory_space=pltpu.VMEM)
    return pl.pallas_call(
        border_kernel,
        in_specs=[vmem] * 4,
        out_specs=[vmem] * 2,
        out_shape=[pltpu.VMEM(cot_a.shape, BF)] * 2,
        input_output_aliases={2: 0, 3: 1},
        compiler_params=pltpu.CompilerParams(vmem_limit_bytes=4 * MIB),
    )(*in_vmem(first, second, cot_a, cot_b))


STEP = 8


def split(cells, planes, spread, row, s):
    spread[s, 8:264, :] = cells[row].astype(F32)
    for c in range(4):
        planes[row, :, 128 * c : 128 * (c + 1)] = spread[s, pl.ds(7 + c, 128, stride=2), :].astype(BF)


def split_all(cells, planes, spread):
    zero = jnp.zeros((8, 128), F32)
    for s in range(spread.shape[0]):
        spread[s, 0:8, :] = zero
        spread[s, 264:272, :] = zero

    for row in range(ROWS + 2):
        split(cells, planes, spread, row, row % spread.shape[0])


def conv(taps, dt, planes, y):
    total = 0.0
    for dy in range(3):
        window = planes[pl.ds(y + 2 - dy, STEP)].reshape(STEP * 128, 512)
        total = total + dot(window, taps[3 * dt + dy])
    return total


def own_cells(planes, y):
    return planes[pl.ds(y + 1, STEP), :, 128:384].reshape(STEP * 128, 256).astype(F32)


def analyze(total):
    total = (0.5 * total).reshape(STEP // 2, 2, 128, 256)
    upper = total[:, 0].reshape(STEP * 64, 256)
    lower = total[:, 1].reshape(STEP * 64, 256)
    a, b, c, d = upper[:, :128], upper[:, 128:], lower[:, :128], lower[:, 128:]
    ab, am, cd, cm = a + b, a - b, c + d, c - d
    return jnp.concatenate([ab + cd, ab - cd, am + cm, am - cm], axis=1).astype(BF)


def rows_of(k, count):
    return slice(k * count, (k + 1) * count)


def add_taps(gk, ft, dt, planes, before):
    cols = planes.reshape((ROWS + 2) * 128, 512)
    for dy in range(3):
        got = dot(ft[...], cols[128 * (2 - dy) : 128 * (ROWS + 2 - dy)])
        for dx in range(3):
            col = 2 - dx
            both = got[0:128, 128 * col : 128 * (col + 1)] + got[128:256, 128 * (col + 1) : 128 * (col + 2)]
            where = slice(128 * (9 * dt + 3 * dy + dx), 128 * (9 * dt + 3 * dy + dx + 1))
            gk[where] = both if before is None else before[where] + both


def add_weights(gw, pairs, before):
    for n, (left, right) in enumerate(pairs):
        part = lax.dot_general(left[...], right[...], (((0,), (0,)), ((), ())), preferred_element_type=F32)
        where = slice(512 * n, 512 * (n + 1))
        gw[where] = part if before is None else before[where] + part


def early_kernel(lat, w1, w2, ker, act, slope, ft_a, cot_a, cot_b, *refs):
    gl_h, part, gk, gw, act_b, slope_b, ft_b, taps, w1t, w2t = refs[:10]
    planes_a, planes_b, spread, gm, gp, gl, sem = refs[10:]
    n_px = gm.shape[0]
    mine = pl.ds(0, n_px)
    turn(w1, w2, ker, taps, w1t, w2t)
    split_all(cot_a, planes_a, spread)
    add_taps(gk, ft_a, 1, planes_a, None)
    split_all(cot_b, planes_b, spread)
    for k in range(ROWS // STEP):
        y = k * STEP
        total = own_cells(planes_a, y) + conv(taps, 1, planes_a, y) + conv(taps, 0, planes_b, y)
        gm[rows_of(k, STEP * 64)] = analyze(total)
    for k in range(ROWS // STEP):
        y = k * STEP
        part[rows_of(k, STEP * 128)] = own_cells(planes_b, y) + conv(taps, 1, planes_b, y)
    gp[...] = (dot(gm[...], w2t[...]) * slope[...].astype(F32)).astype(BF)
    gl[...] = (gm[...].astype(F32) + dot(gp[...], w1t[...])).astype(BF)
    out = pltpu.make_async_copy(gl, gl_h.at[mine], sem)
    out.start()
    add_weights(gw, ((lat.at[mine], gp), (act, gm)), None)
    project(lat[n_px : 2 * n_px], w1, w2, act_b, slope_b, ft_b)
    add_taps(gk, ft_a, 0, planes_b, None)
    add_taps(gk, ft_b, 1, planes_b, gk)
    out.wait()


def late_kernel(lat, act, slope, ft, taps, w2t, cells, part, sumk, sumw, gm, gp, keep, send, *scratch):
    planes, spread, gk, gw = scratch
    n_px = gm.shape[0]
    mine = pl.ds(n_px, n_px)
    split_all(cells, planes, spread)

    for k in range(ROWS // STEP):
        total = part[rows_of(k, STEP * 128)] + conv(taps, 0, planes, k * STEP)
        gm[rows_of(k, STEP * 64)] = analyze(total)
    gp[...] = (dot(gm[...], w2t[...]) * slope[...].astype(F32)).astype(BF)
    gk[128 * 9 :] = sumk[128 * 9 :]
    add_taps(gk, ft, 0, planes, sumk)
    add_weights(gw, ((lat.at[mine], gp), (act, gm)), sumw)
    ids = block_ids()
    for r in range(8):
        packed = (keep, send)[r // 4].at[r % 4]
        b = ids[r]
        for lane in range(4):
            packed[128 * lane : 128 * (lane + 1), :] = gw[
                pl.ds(pl.multiple_of(b * 128, 128), 128), 128 * lane : 128 * (lane + 1)
            ].astype(BF)
        packed[512:800, :] = gk[pl.ds(pl.multiple_of(b * 288, 32), 288), :].astype(BF)


def last_kernel(gm, gp, w1t, _, gl_h, gl, sem):
    n_px = gm.shape[0]
    gl[...] = (gm[...].astype(F32) + dot(gp[...], w1t[...])).astype(BF)
    out = pltpu.make_async_copy(gl, gl_h.at[pl.ds(n_px, n_px)], sem)
    out.start()
    out.wait()


PLANES = (ROWS + 2, 128, 512)
SUMS = [(2304, 128), (1024, 512)]
SPREAD = (2, 272, 128)


def early(lat, *rest):
    n_px = lat.shape[0] // 2
    ops = in_vmem(lat, *rest)
    shapes = [pltpu.VMEM(shape, F32) for shape in [(ROWS * 128, 256)] + SUMS]
    shapes += [pltpu.VMEM(shape, BF) for shape in frame_shapes(n_px) + [(6, 512, 256), (512, 512), (512, 512)]]
    return pl.pallas_call(
        early_kernel,
        in_specs=[VMEM_SPEC] * len(ops),
        out_specs=[ANY_SPEC] + [VMEM_SPEC] * len(shapes),
        out_shape=[pltpu.HBM(lat.shape, BF)] + shapes,
        scratch_shapes=[pltpu.VMEM(PLANES, BF)] * 2
        + [pltpu.VMEM(SPREAD, F32)]
        + [pltpu.VMEM((n_px, 512), BF)] * 3
        + [pltpu.SemaphoreType.DMA],
        cost_estimate=pl.CostEstimate(flops=12 << 30, bytes_accessed=16 * MIB, transcendentals=0),
        compiler_params=pltpu.CompilerParams(vmem_limit_bytes=24 * MIB),
    )(*ops)


def late(lat, act, slope, ft, taps, w2t, cells, part, gk, gw):
    half = (lat.shape[0] // 2, 512)
    ops = in_vmem(lat, act, slope, ft, taps, w2t, cells, part, gk, gw)
    return pl.pallas_call(
        late_kernel,
        in_specs=[VMEM_SPEC] * len(ops),
        out_specs=[VMEM_SPEC] * 4,
        out_shape=[pltpu.VMEM(half, BF)] * 2 + [pltpu.VMEM((4, 800, 128), BF)] * 2,
        scratch_shapes=[pltpu.VMEM(PLANES, BF), pltpu.VMEM(SPREAD, F32)]
        + [pltpu.VMEM(shape, F32) for shape in SUMS],
        cost_estimate=pl.CostEstimate(flops=6 << 30, bytes_accessed=16 * MIB, transcendentals=0),
        compiler_params=pltpu.CompilerParams(vmem_limit_bytes=24 * MIB),
    )(*ops)


def last(gm, gp, w1t, grad):
    return pl.pallas_call(
        last_kernel,
        in_specs=[VMEM_SPEC] * 3 + [ANY_SPEC],
        out_specs=ANY_SPEC,
        out_shape=pltpu.HBM(grad.shape, BF),
        input_output_aliases={3: 0},
        scratch_shapes=[pltpu.VMEM(gm.shape, BF), pltpu.SemaphoreType.DMA],
        cost_estimate=pl.CostEstimate(flops=1 << 29, bytes_accessed=4 * MIB, transcendentals=0),
        compiler_params=pltpu.CompilerParams(vmem_limit_bytes=8 * MIB),
    )(*in_vmem(gm, gp, w1t), *in_hbm(grad))


def unpack_kernel(side, *refs):
    if side:
        (other, *_), refs = refs[:4], refs[4:]
        pieces = [other.at[r] for r in range(4)]
    else:
        pieces, refs = refs[:4], refs[4:]
    first_h, second_h, gk_h, gw, gk, sems = refs
    copies = []
    ids = block_ids()[4 * side : 4 * side + 4]
    for r in range(4):
        b, piece = ids[r], pieces[r]
        down = pl.ds(pl.multiple_of((b % 4) * 128, 128), 128)
        low = pl.ds(pl.multiple_of(b * 288, 32), 288)
        for lane in range(4):
            cols = slice(128 * lane, 128 * (lane + 1))
            gw[r, :, cols] = piece[cols, :].astype(F32)
        gk[r] = piece[512:800, :].astype(F32)
        copies.append(pltpu.make_async_copy(gk.at[r], gk_h.at[low], sems.at[0, r]))
        copies[-1].start()
        to_first = pltpu.make_async_copy(gw.at[r], first_h.at[down], sems.at[1, r])
        to_second = pltpu.make_async_copy(gw.at[r], second_h.at[down], sems.at[1, r])
        pl.when(b < 4)(to_first.start)
        pl.when(b >= 4)(to_second.start)
        copies.append(to_first)
    for copy in copies:
        copy.wait()


def unpack(side, pieces, outs=()):
    return pl.pallas_call(
        functools.partial(unpack_kernel, side),
        in_specs=[VMEM_SPEC] * len(pieces) + [ANY_SPEC] * len(outs),
        out_specs=[ANY_SPEC] * 3,
        out_shape=[pltpu.HBM(shape, F32) for shape in ((512, 512), (512, 512), (2304, 128))],
        input_output_aliases={1 + n: n for n in range(len(outs))},
        scratch_shapes=[
            pltpu.VMEM((4, 128, 512), F32),
            pltpu.VMEM((4, 288, 128), F32),
            pltpu.SemaphoreType.DMA((2, 4)),
        ],
        cost_estimate=pl.CostEstimate(flops=1 << 20, bytes_accessed=3 * MIB, transcendentals=0),
        compiler_params=pltpu.CompilerParams(vmem_limit_bytes=8 * MIB),
    )(*pieces, *in_hbm(*outs))


BOTH = ("ha", "ta")


def coords(device):
    ha, ta = divmod(device, 16)
    return [(ta // 2 % 2) * 2 + ha % 2, ha // 2, ta // 4, ta % 2]


def device_at(x, y, z, core):
    return (y * 2 + x % 2) * 16 + z * 4 + (x // 2) * 2 + core


def along(axes, move):
    pairs = []
    for device in range(128):
        place = coords(device)
        axis = axes[place[3]]
        place[axis] = move(place[axis])
        pairs.append((device, device_at(*place)))
    return pairs


def step_by(count):
    return lambda place: (place + count) % 4


def rounded(value):
    return lax.reduce_precision(value, 8, 7).astype(BF)


def swap(value):
    return lax.ppermute(value, BOTH, [(i, i ^ 1) for i in range(128)])


def trade(near, far, last, axes):
    across = lax.ppermute(far, BOTH, along(axes, step_by(2)))
    before = lax.ppermute(near, BOTH, along(axes, step_by(1)))
    after = lax.ppermute(last, BOTH, along(axes, step_by(3)))
    return before, across, after


def add4(own, before, across, after):
    return rounded((own.astype(F32) + across.astype(F32)) + (before.astype(F32) + after.astype(F32)))


def place():
    ha, ta = lax.axis_index("ha"), lax.axis_index("ta")
    return (ta // 2 % 2) * 2 + ha % 2, ha // 2, ta // 4, ta % 2


def block_ids():
    _, y, z, core = place()
    ids = []
    for other in range(2):
        owner = core ^ other
        start = jnp.where(owner == 0, z, y)
        ids += [owner * 4 + (start + k) % 4 for k in range(4)]
    return ids


def add2(a, b):
    return rounded(a.astype(F32) + b.astype(F32))


def sum_all(keep, got):
    parts = [add2(keep[k], got[k]) for k in range(4)]
    own = add4(parts[0], *trade(*parts[1:], (2, 1)))
    own = add4(own, *trade(own, own, own, (1, 0)))
    own = add4(own, *trade(own, own, own, (0, 2)))
    before, across, after = trade(own, own, own, (2, 1))
    other = swap(jnp.stack([own, after, across, before]))
    outs = unpack(0, (own, after, across, before))
    return unpack(1, (other,), outs)


def neighbour(value, axis, step):
    count = lax.axis_size(axis)
    return lax.ppermute(value, axis, [(i, i + step) for i in range(count) if 0 <= i + step < count])


def meetings(count):
    inner = [(i, i ^ 1) for i in range(count)]
    outer = [(i, i + 1 if i % 2 else i - 1) for i in range(1, count - 1)]
    return inner, outer


def shards(latent, w_first, w_second, kernel, cotangent):
    width = latent.shape[-1]
    flat = latent.reshape(-1, width)
    odd = lax.axis_index("ha") % 2
    top, bottom = cotangent[:, 0], cotangent[:, -1]
    meet = meetings(lax.axis_size("ha"))
    inner = lax.ppermute(jnp.where(odd == 1, top, bottom), "ha", meet[0])
    outer = lax.ppermute(jnp.where(odd == 1, bottom, top), "ha", meet[1])
    lat, w1, w2, ker, cot_a, cot_b, act_a, slope_a, ft_a = first(flat, w_first, w_second, kernel, cotangent)
    cot_a, cot_b = border(inner, outer, cot_a, cot_b)
    later = neighbour(cot_a, "ta", -1)
    middle = early(lat, w1, w2, ker, act_a, slope_a, ft_a, cot_a, cot_b)
    grad, part, gk, gw, act_b, slope_b, ft_b, taps, w1t, w2t = middle
    gm, gp, keep, send = late(lat, act_b, slope_b, ft_b, taps, w2t, later, part, gk, gw)
    got = swap(send)
    grad = last(gm, gp, w1t, grad)
    got, grad = lax.optimization_barrier((got, grad))
    grad_first, grad_second, gk = sum_all(keep, got)
    return grad.reshape(latent.shape), grad_first, grad_second, gk.reshape(kernel.shape)


def solution(mesh):
    return jax.shard_map(
        shards,
        mesh=mesh,
        in_specs=(P("ta", "ha", None, None), P(), P(), P(), P("ta", "ha", None, None)),
        out_specs=(P("ta", "ha", None, None), P(), P(), P()),
        check_vma=False,
    )
```

```python
import functools
import jax
import jax.numpy as jnp
from jax import lax
from jax.experimental import pallas as pl
from jax.experimental.pallas import tpu as pltpu
from jax.sharding import PartitionSpec as P

BF, F32 = jnp.bfloat16, jnp.float32
ROWS = 16
MIB = 1 << 20


def in_hbm(*arrays):
    return [pltpu.with_memory_space_constraint(array, pltpu.HBM) for array in arrays]


def in_vmem(*arrays):
    return [pltpu.with_memory_space_constraint(array, pltpu.VMEM) for array in arrays]


def dot(a, b):
    return jnp.dot(a, b, preferred_element_type=F32)


def project(x, w1, w2, act, slope, ft):
    pre = dot(x, w1[...])
    sig = 0.5 * jnp.tanh(0.5 * pre) + 0.5
    hidden = pre * sig
    slope[...] = (sig + hidden * (1.0 - sig)).astype(BF)
    hidden = hidden.astype(BF)
    act[...] = hidden
    mixed = 0.5 * (x.astype(F32) + dot(hidden, w2[...]))
    ll, lh, hl, hh = (mixed[:, 128 * b : 128 * (b + 1)] for b in range(4))
    s, d, t, u = ll + lh, ll - lh, hl + hh, hl - hh
    for i in range(x.shape[0] // 128):
        px = slice(128 * i, 128 * (i + 1))
        for p, (m, n) in enumerate(((s, t), (d, u))):
            row = 2 * i + p
            lanes = slice(128 * row, 128 * (row + 1))
            ft[0:128, lanes] = (m[px] + n[px]).astype(BF).T
            ft[128:256, lanes] = (m[px] - n[px]).astype(BF).T


def first_kernel(lat_h, w1_h, w2_h, k_h, cot_h, lat, w1, w2, ker, cot_a, cot_b, act, slope, ft, sems):
    n_px = act.shape[0]
    pairs = [(w1_h, w1), (lat_h.at[pl.ds(0, n_px)], lat.at[pl.ds(0, n_px)]), (w2_h, w2)]
    pairs += [(cot_h.at[n], dst.at[pl.ds(1, ROWS)]) for n, dst in enumerate((cot_a, cot_b))]
    pairs += [(lat_h.at[pl.ds(n_px, n_px)], lat.at[pl.ds(n_px, n_px)]), (k_h, ker)]
    copies = [pltpu.make_async_copy(src, dst, sems.at[n]) for n, (src, dst) in enumerate(pairs)]
    for copy in copies:
        copy.start()
    for copy in copies[:3]:
        copy.wait()
    project(lat[0:n_px], w1, w2, act, slope, ft)
    for copy in copies[3:]:
        copy.wait()


def turn(w1, w2, ker, taps, w1t, w2t):
    w1t[...] = w1[...].T
    w2t[...] = w2[...].T
    for t in range(6):
        for q in range(2):
            col = 3 * (1 - q)
            taps[t, 128 * col : 128 * (col + 1), 128 * q : 128 * (q + 1)] = jnp.zeros((128, 128), BF)
        for dx in range(3):
            tap = ker[3 * t + dx].T
            for q in range(2):
                col = 2 - dx + q
                taps[t, 128 * col : 128 * (col + 1), 128 * q : 128 * (q + 1)] = tap


VMEM_SPEC = pl.BlockSpec(memory_space=pltpu.VMEM)
ANY_SPEC = pl.BlockSpec(memory_space=pl.ANY)


def frame_shapes(n_px):
    return [(n_px, 512), (n_px, 512), (256, 2 * n_px)]


def first(latent, w1, w2, kernel, cotangent):
    n = latent.shape[0]
    frame = (ROWS + 2,) + cotangent.shape[2:]
    shapes = [(n, 512), (512, 512), (512, 512), (18, 128, 128), frame, frame] + frame_shapes(n // 2)
    return pl.pallas_call(
        first_kernel,
        in_specs=[ANY_SPEC] * 5,
        out_specs=[VMEM_SPEC] * len(shapes),
        out_shape=[pltpu.VMEM(shape, BF) for shape in shapes],
        scratch_shapes=[pltpu.SemaphoreType.DMA((7,))],
        cost_estimate=pl.CostEstimate(flops=4 * n * 512 * 512, bytes_accessed=8 * MIB, transcendentals=n * 256),
        compiler_params=pltpu.CompilerParams(vmem_limit_bytes=16 * MIB),
    )(*in_hbm(latent, w1, w2, kernel.reshape(18, 128, 128), cotangent))


def border_kernel(first, second, _, __, cot_a, cot_b):
    odd = lax.axis_index("ha") % 2
    for upper, lower, here in ((second, first, odd == 0), (first, second, odd == 1)):

        @pl.when(here)
        def _():
            for n, cot in enumerate((cot_a, cot_b)):
                cot[0] = upper[n]
                cot[ROWS + 1] = lower[n]


def border(first, second, cot_a, cot_b):
    vmem = pl.BlockSpec(memory_space=pltpu.VMEM)
    return pl.pallas_call(
        border_kernel,
        in_specs=[vmem] * 4,
        out_specs=[vmem] * 2,
        out_shape=[pltpu.VMEM(cot_a.shape, BF)] * 2,
        input_output_aliases={2: 0, 3: 1},
        compiler_params=pltpu.CompilerParams(vmem_limit_bytes=4 * MIB),
    )(*in_vmem(first, second, cot_a, cot_b))


STEP = 4


def split(cells, planes, spread, row, s):
    spread[s, 8:264, :] = cells[row].astype(F32)
    for c in range(4):
        planes[row, :, 128 * c : 128 * (c + 1)] = spread[s, pl.ds(7 + c, 128, stride=2), :].astype(BF)


def split_all(cells, planes, spread):
    zero = jnp.zeros((8, 128), F32)
    for s in range(spread.shape[0]):
        spread[s, 0:8, :] = zero
        spread[s, 264:272, :] = zero

    for row in range(ROWS + 2):
        split(cells, planes, spread, row, row % spread.shape[0])


def conv(taps, dt, planes, y):
    total = 0.0
    for dy in range(3):
        window = planes[pl.ds(y + 2 - dy, STEP)].reshape(STEP * 128, 512)
        total = total + dot(window, taps[3 * dt + dy])
    return total


def own_cells(planes, y):
    return planes[pl.ds(y + 1, STEP), :, 128:384].reshape(STEP * 128, 256).astype(F32)


def analyze(total):
    total = (0.5 * total).reshape(STEP // 2, 2, 128, 256)
    upper = total[:, 0].reshape(STEP * 64, 256)
    lower = total[:, 1].reshape(STEP * 64, 256)
    a, b, c, d = upper[:, :128], upper[:, 128:], lower[:, :128], lower[:, 128:]
    ab, am, cd, cm = a + b, a - b, c + d, c - d
    return jnp.concatenate([ab + cd, ab - cd, am + cm, am - cm], axis=1).astype(BF)


def rows_of(k, count):
    return slice(k * count, (k + 1) * count)


def add_taps(gk, ft, dt, planes, before):
    cols = planes.reshape((ROWS + 2) * 128, 512)
    for dy in range(3):
        got = dot(ft[...], cols[128 * (2 - dy) : 128 * (ROWS + 2 - dy)])
        for dx in range(3):
            col = 2 - dx
            both = got[0:128, 128 * col : 128 * (col + 1)] + got[128:256, 128 * (col + 1) : 128 * (col + 2)]
            where = slice(128 * (9 * dt + 3 * dy + dx), 128 * (9 * dt + 3 * dy + dx + 1))
            gk[where] = both if before is None else before[where] + both


def add_weights(gw, pairs, before):
    for n, (left, right) in enumerate(pairs):
        part = lax.dot_general(left[...], right[...], (((0,), (0,)), ((), ())), preferred_element_type=F32)
        where = slice(512 * n, 512 * (n + 1))
        gw[where] = part if before is None else before[where] + part


def early_kernel(lat, w1, w2, ker, act, slope, ft_a, cot_a, cot_b, *refs):
    gl_h, part, gk, gw, act_b, slope_b, ft_b, taps, w1t, w2t = refs[:10]
    planes_a, planes_b, spread, gm, gp, gl, sem = refs[10:]
    n_px = gm.shape[0]
    mine = pl.ds(0, n_px)
    turn(w1, w2, ker, taps, w1t, w2t)
    split_all(cot_a, planes_a, spread)
    add_taps(gk, ft_a, 1, planes_a, None)
    split_all(cot_b, planes_b, spread)
    for k in range(ROWS // STEP):
        y = k * STEP
        total = own_cells(planes_a, y) + conv(taps, 1, planes_a, y) + conv(taps, 0, planes_b, y)
        gm[rows_of(k, STEP * 64)] = analyze(total)
    for k in range(ROWS // STEP):
        y = k * STEP
        part[rows_of(k, STEP * 128)] = own_cells(planes_b, y) + conv(taps, 1, planes_b, y)
    gp[...] = (dot(gm[...], w2t[...]) * slope[...].astype(F32)).astype(BF)
    gl[...] = (gm[...].astype(F32) + dot(gp[...], w1t[...])).astype(BF)
    out = pltpu.make_async_copy(gl, gl_h.at[mine], sem)
    out.start()
    add_weights(gw, ((lat.at[mine], gp), (act, gm)), None)
    project(lat[n_px : 2 * n_px], w1, w2, act_b, slope_b, ft_b)
    add_taps(gk, ft_a, 0, planes_b, None)
    add_taps(gk, ft_b, 1, planes_b, gk)
    out.wait()


def late_kernel(lat, act, slope, ft, taps, w2t, cells, part, sumk, sumw, gm, gp, keep, send, *scratch):
    planes, spread, gk, gw = scratch
    n_px = gm.shape[0]
    mine = pl.ds(n_px, n_px)
    split_all(cells, planes, spread)

    for k in range(ROWS // STEP):
        total = part[rows_of(k, STEP * 128)] + conv(taps, 0, planes, k * STEP)
        gm[rows_of(k, STEP * 64)] = analyze(total)
    gp[...] = (dot(gm[...], w2t[...]) * slope[...].astype(F32)).astype(BF)
    add_taps(gk, ft, 0, planes, sumk)
    add_weights(gw, ((lat.at[mine], gp), (act, gm)), sumw)
    ids = block_ids()
    for r in range(8):
        packed = (keep, send)[r // 4].at[r % 4]
        b = ids[r]
        for lane in range(4):
            packed[128 * lane : 128 * (lane + 1), :] = gw[
                pl.ds(pl.multiple_of(b * 128, 128), 128), 128 * lane : 128 * (lane + 1)
            ].astype(BF)
        new = gk[pl.ds(pl.multiple_of((b % 4) * 288, 32), 288), :]
        old = sumk[pl.ds(pl.multiple_of(b * 288, 32), 288), :]
        packed[512:800, :] = jnp.where(b < 4, new, old).astype(BF)


def last_kernel(gm, gp, w1t, _, gl_h, gl, sem):
    n_px = gm.shape[0]
    gl[...] = (gm[...].astype(F32) + dot(gp[...], w1t[...])).astype(BF)
    out = pltpu.make_async_copy(gl, gl_h.at[pl.ds(n_px, n_px)], sem)
    out.start()
    out.wait()


PLANES = (ROWS + 2, 128, 512)
SUMS = [(2304, 128), (1024, 512)]
SPREAD = (2, 272, 128)


def early(lat, *rest):
    n_px = lat.shape[0] // 2
    ops = in_vmem(lat, *rest)
    shapes = [pltpu.VMEM(shape, F32) for shape in [(ROWS * 128, 256)] + SUMS]
    shapes += [pltpu.VMEM(shape, BF) for shape in frame_shapes(n_px) + [(6, 512, 256), (512, 512), (512, 512)]]
    return pl.pallas_call(
        early_kernel,
        in_specs=[VMEM_SPEC] * len(ops),
        out_specs=[ANY_SPEC] + [VMEM_SPEC] * len(shapes),
        out_shape=[pltpu.HBM(lat.shape, BF)] + shapes,
        scratch_shapes=[pltpu.VMEM(PLANES, BF)] * 2
        + [pltpu.VMEM(SPREAD, F32)]
        + [pltpu.VMEM((n_px, 512), BF)] * 3
        + [pltpu.SemaphoreType.DMA],
        cost_estimate=pl.CostEstimate(flops=12 << 30, bytes_accessed=16 * MIB, transcendentals=0),
        compiler_params=pltpu.CompilerParams(vmem_limit_bytes=24 * MIB),
    )(*ops)


def late(lat, act, slope, ft, taps, w2t, cells, part, gk, gw):
    half = (lat.shape[0] // 2, 512)
    ops = in_vmem(lat, act, slope, ft, taps, w2t, cells, part, gk, gw)
    return pl.pallas_call(
        late_kernel,
        in_specs=[VMEM_SPEC] * len(ops),
        out_specs=[VMEM_SPEC] * 4,
        out_shape=[pltpu.VMEM(half, BF)] * 2 + [pltpu.VMEM((4, 800, 128), BF)] * 2,
        scratch_shapes=[pltpu.VMEM(PLANES, BF), pltpu.VMEM(SPREAD, F32)]
        + [pltpu.VMEM(shape, F32) for shape in SUMS],
        cost_estimate=pl.CostEstimate(flops=6 << 30, bytes_accessed=16 * MIB, transcendentals=0),
        compiler_params=pltpu.CompilerParams(vmem_limit_bytes=24 * MIB),
    )(*ops)


def last(gm, gp, w1t, grad):
    return pl.pallas_call(
        last_kernel,
        in_specs=[VMEM_SPEC] * 3 + [ANY_SPEC],
        out_specs=ANY_SPEC,
        out_shape=pltpu.HBM(grad.shape, BF),
        input_output_aliases={3: 0},
        scratch_shapes=[pltpu.VMEM(gm.shape, BF), pltpu.SemaphoreType.DMA],
        cost_estimate=pl.CostEstimate(flops=1 << 29, bytes_accessed=4 * MIB, transcendentals=0),
        compiler_params=pltpu.CompilerParams(vmem_limit_bytes=8 * MIB),
    )(*in_vmem(gm, gp, w1t), *in_hbm(grad))


def unpack_kernel(side, *refs):
    if side:
        (other, *_), refs = refs[:4], refs[4:]
        pieces = [other.at[r] for r in range(4)]
    else:
        pieces, refs = refs[:4], refs[4:]
    first_h, second_h, gk_h, gw, gk, sems = refs
    copies = []
    ids = block_ids()[4 * side : 4 * side + 4]
    for r in range(4):
        b, piece = ids[r], pieces[r]
        down = pl.ds(pl.multiple_of((b % 4) * 128, 128), 128)
        low = pl.ds(pl.multiple_of(b * 288, 32), 288)
        for lane in range(4):
            cols = slice(128 * lane, 128 * (lane + 1))
            gw[r, :, cols] = piece[cols, :].astype(F32)
        gk[r] = piece[512:800, :].astype(F32)
        copies.append(pltpu.make_async_copy(gk.at[r], gk_h.at[low], sems.at[0, r]))
        copies[-1].start()
        to_first = pltpu.make_async_copy(gw.at[r], first_h.at[down], sems.at[1, r])
        to_second = pltpu.make_async_copy(gw.at[r], second_h.at[down], sems.at[1, r])
        pl.when(b < 4)(to_first.start)
        pl.when(b >= 4)(to_second.start)
        copies.append(to_first)
    for copy in copies:
        copy.wait()


def unpack(side, pieces, outs=()):
    return pl.pallas_call(
        functools.partial(unpack_kernel, side),
        in_specs=[VMEM_SPEC] * len(pieces) + [ANY_SPEC] * len(outs),
        out_specs=[ANY_SPEC] * 3,
        out_shape=[pltpu.HBM(shape, F32) for shape in ((512, 512), (512, 512), (2304, 128))],
        input_output_aliases={1 + n: n for n in range(len(outs))},
        scratch_shapes=[
            pltpu.VMEM((4, 128, 512), F32),
            pltpu.VMEM((4, 288, 128), F32),
            pltpu.SemaphoreType.DMA((2, 4)),
        ],
        cost_estimate=pl.CostEstimate(flops=1 << 20, bytes_accessed=3 * MIB, transcendentals=0),
        compiler_params=pltpu.CompilerParams(vmem_limit_bytes=8 * MIB),
    )(*pieces, *in_hbm(*outs))


BOTH = ("ha", "ta")


def coords(device):
    ha, ta = divmod(device, 16)
    return [(ta // 2 % 2) * 2 + ha % 2, ha // 2, ta // 4, ta % 2]


def device_at(x, y, z, core):
    return (y * 2 + x % 2) * 16 + z * 4 + (x // 2) * 2 + core


def along(axes, move):
    pairs = []
    for device in range(128):
        place = coords(device)
        axis = axes[place[3]]
        place[axis] = move(place[axis])
        pairs.append((device, device_at(*place)))
    return pairs


def step_by(count):
    return lambda place: (place + count) % 4


def rounded(value):
    return lax.reduce_precision(value, 8, 7).astype(BF)


def swap(value):
    return lax.ppermute(value, BOTH, [(i, i ^ 1) for i in range(128)])


def trade(near, far, last, axes):
    across = lax.ppermute(far, BOTH, along(axes, step_by(2)))
    before = lax.ppermute(near, BOTH, along(axes, step_by(1)))
    after = lax.ppermute(last, BOTH, along(axes, step_by(3)))
    return before, across, after


def add4(own, before, across, after):
    return rounded((own.astype(F32) + across.astype(F32)) + (before.astype(F32) + after.astype(F32)))


def place():
    ha, ta = lax.axis_index("ha"), lax.axis_index("ta")
    return (ta // 2 % 2) * 2 + ha % 2, ha // 2, ta // 4, ta % 2


def block_ids():
    _, y, z, core = place()
    ids = []
    for other in range(2):
        owner = core ^ other
        start = jnp.where(owner == 0, z, y)
        ids += [owner * 4 + (start + k) % 4 for k in range(4)]
    return ids


def add2(a, b):
    return rounded(a.astype(F32) + b.astype(F32))


def sum_all(keep, got):
    parts = [add2(keep[k], got[k]) for k in range(4)]
    own = add4(parts[0], *trade(*parts[1:], (2, 1)))
    own = add4(own, *trade(own, own, own, (1, 0)))
    own = add4(own, *trade(own, own, own, (0, 2)))
    before, across, after = trade(own, own, own, (2, 1))
    other = swap(jnp.stack([own, after, across, before]))
    outs = unpack(0, (own, after, across, before))
    return unpack(1, (other,), outs)


def neighbour(value, axis, step):
    count = lax.axis_size(axis)
    return lax.ppermute(value, axis, [(i, i + step) for i in range(count) if 0 <= i + step < count])


def meetings(count):
    inner = [(i, i ^ 1) for i in range(count)]
    outer = [(i, i + 1 if i % 2 else i - 1) for i in range(1, count - 1)]
    return inner, outer


def shards(latent, w_first, w_second, kernel, cotangent):
    width = latent.shape[-1]
    flat = latent.reshape(-1, width)
    odd = lax.axis_index("ha") % 2
    top, bottom = cotangent[:, 0], cotangent[:, -1]
    meet = meetings(lax.axis_size("ha"))
    inner = lax.ppermute(jnp.where(odd == 1, top, bottom), "ha", meet[0])
    outer = lax.ppermute(jnp.where(odd == 1, bottom, top), "ha", meet[1])
    lat, w1, w2, ker, cot_a, cot_b, act_a, slope_a, ft_a = first(flat, w_first, w_second, kernel, cotangent)
    cot_a, cot_b = border(inner, outer, cot_a, cot_b)
    later = neighbour(cot_a, "ta", -1)
    middle = early(lat, w1, w2, ker, act_a, slope_a, ft_a, cot_a, cot_b)
    grad, part, gk, gw, act_b, slope_b, ft_b, taps, w1t, w2t = middle
    gm, gp, keep, send = late(lat, act_b, slope_b, ft_b, taps, w2t, later, part, gk, gw)
    got = swap(send)
    grad = last(gm, gp, w1t, grad)
    got, grad = lax.optimization_barrier((got, grad))
    grad_first, grad_second, gk = sum_all(keep, got)
    return grad.reshape(latent.shape), grad_first, grad_second, gk.reshape(kernel.shape)


def solution(mesh):
    return jax.shard_map(
        shards,
        mesh=mesh,
        in_specs=(P("ta", "ha", None, None), P(), P(), P(), P("ta", "ha", None, None)),
        out_specs=(P("ta", "ha", None, None), P(), P(), P()),
        check_vma=False,
    )
```

```python
import functools
import jax
import jax.numpy as jnp
from jax import lax
from jax.experimental import pallas as pl
from jax.experimental.pallas import tpu as pltpu
from jax.sharding import PartitionSpec as P

BF, F32 = jnp.bfloat16, jnp.float32
ROWS = 16
MIB = 1 << 20


def in_hbm(*arrays):
    return [pltpu.with_memory_space_constraint(array, pltpu.HBM) for array in arrays]


def in_vmem(*arrays):
    return [pltpu.with_memory_space_constraint(array, pltpu.VMEM) for array in arrays]


def dot(a, b):
    return jnp.dot(a, b, preferred_element_type=F32)


def project(x, w1, w2, act, slope, ft):
    pre = dot(x, w1[...])
    sig = 0.5 * jnp.tanh(0.5 * pre) + 0.5
    hidden = pre * sig
    slope[...] = (sig + hidden * (1.0 - sig)).astype(BF)
    hidden = hidden.astype(BF)
    act[...] = hidden
    mixed = 0.5 * (x.astype(F32) + dot(hidden, w2[...]))
    ll, lh, hl, hh = (mixed[:, 128 * b : 128 * (b + 1)] for b in range(4))
    s, d, t, u = ll + lh, ll - lh, hl + hh, hl - hh
    for i in range(x.shape[0] // 128):
        px = slice(128 * i, 128 * (i + 1))
        for p, (m, n) in enumerate(((s, t), (d, u))):
            row = 2 * i + p
            lanes = slice(128 * row, 128 * (row + 1))
            ft[0:128, lanes] = (m[px] + n[px]).astype(BF).T
            ft[128:256, lanes] = (m[px] - n[px]).astype(BF).T


def first_kernel(lat_h, w1_h, w2_h, k_h, cot_h, lat, w1, w2, ker, cot_a, cot_b, act, slope, ft, sems):
    n_px = act.shape[0]
    pairs = [(w1_h, w1), (lat_h.at[pl.ds(0, n_px)], lat.at[pl.ds(0, n_px)]), (w2_h, w2)]
    pairs += [(cot_h.at[n], dst.at[pl.ds(1, ROWS)]) for n, dst in enumerate((cot_a, cot_b))]
    pairs += [(lat_h.at[pl.ds(n_px, n_px)], lat.at[pl.ds(n_px, n_px)]), (k_h, ker)]
    copies = [pltpu.make_async_copy(src, dst, sems.at[n]) for n, (src, dst) in enumerate(pairs)]
    for copy in copies:
        copy.start()
    for copy in copies[:3]:
        copy.wait()
    project(lat[0:n_px], w1, w2, act, slope, ft)
    for copy in copies[3:]:
        copy.wait()


def turn(w1, w2, ker, taps, w1t, w2t):
    w1t[...] = w1[...].T
    w2t[...] = w2[...].T
    for t in range(6):
        for q in range(2):
            col = 3 * (1 - q)
            taps[t, 128 * col : 128 * (col + 1), 128 * q : 128 * (q + 1)] = jnp.zeros((128, 128), BF)
        for dx in range(3):
            tap = ker[3 * t + dx].T
            for q in range(2):
                col = 2 - dx + q
                taps[t, 128 * col : 128 * (col + 1), 128 * q : 128 * (q + 1)] = tap


VMEM_SPEC = pl.BlockSpec(memory_space=pltpu.VMEM)
ANY_SPEC = pl.BlockSpec(memory_space=pl.ANY)


def frame_shapes(n_px):
    return [(n_px, 512), (n_px, 512), (256, 2 * n_px)]


def first(latent, w1, w2, kernel, cotangent):
    n = latent.shape[0]
    frame = (ROWS + 2,) + cotangent.shape[2:]
    shapes = [(n, 512), (512, 512), (512, 512), (18, 128, 128), frame, frame] + frame_shapes(n // 2)
    return pl.pallas_call(
        first_kernel,
        in_specs=[ANY_SPEC] * 5,
        out_specs=[VMEM_SPEC] * len(shapes),
        out_shape=[pltpu.VMEM(shape, BF) for shape in shapes],
        scratch_shapes=[pltpu.SemaphoreType.DMA((7,))],
        cost_estimate=pl.CostEstimate(flops=4 * n * 512 * 512, bytes_accessed=8 * MIB, transcendentals=n * 256),
        compiler_params=pltpu.CompilerParams(vmem_limit_bytes=16 * MIB),
    )(*in_hbm(latent, w1, w2, kernel.reshape(18, 128, 128), cotangent))


def border_kernel(first, second, _, __, cot_a, cot_b):
    odd = lax.axis_index("ha") % 2
    for upper, lower, here in ((second, first, odd == 0), (first, second, odd == 1)):

        @pl.when(here)
        def _():
            for n, cot in enumerate((cot_a, cot_b)):
                cot[0] = upper[n]
                cot[ROWS + 1] = lower[n]


def border(first, second, cot_a, cot_b):
    vmem = pl.BlockSpec(memory_space=pltpu.VMEM)
    return pl.pallas_call(
        border_kernel,
        in_specs=[vmem] * 4,
        out_specs=[vmem] * 2,
        out_shape=[pltpu.VMEM(cot_a.shape, BF)] * 2,
        input_output_aliases={2: 0, 3: 1},
        compiler_params=pltpu.CompilerParams(vmem_limit_bytes=4 * MIB),
    )(*in_vmem(first, second, cot_a, cot_b))


STEP = 4


def split(cells, planes, spread, row, s):
    spread[s, 8:264, :] = cells[row].astype(F32)
    for c in range(4):
        planes[row, :, 128 * c : 128 * (c + 1)] = spread[s, pl.ds(7 + c, 128, stride=2), :].astype(BF)


def split_all(cells, planes, spread):
    zero = jnp.zeros((8, 128), F32)
    for s in range(spread.shape[0]):
        spread[s, 0:8, :] = zero
        spread[s, 264:272, :] = zero

    for row in range(ROWS + 2):
        split(cells, planes, spread, row, row % spread.shape[0])


def conv(taps, dt, planes, y):
    total = 0.0
    for dy in range(3):
        window = planes[pl.ds(y + 2 - dy, STEP)].reshape(STEP * 128, 512)
        total = total + dot(window, taps[3 * dt + dy])
    return total


def own_cells(planes, y):
    return planes[pl.ds(y + 1, STEP), :, 128:384].reshape(STEP * 128, 256).astype(F32)


def analyze(total):
    total = (0.5 * total).reshape(STEP // 2, 2, 128, 256)
    upper = total[:, 0].reshape(STEP * 64, 256)
    lower = total[:, 1].reshape(STEP * 64, 256)
    a, b, c, d = upper[:, :128], upper[:, 128:], lower[:, :128], lower[:, 128:]
    ab, am, cd, cm = a + b, a - b, c + d, c - d
    return jnp.concatenate([ab + cd, ab - cd, am + cm, am - cm], axis=1).astype(BF)


def rows_of(k, count):
    return slice(k * count, (k + 1) * count)


def add_taps(gk, ft, dt, planes, before):
    cols = planes.reshape((ROWS + 2) * 128, 512)
    for dy in range(3):
        got = dot(ft[...], cols[128 * (2 - dy) : 128 * (ROWS + 2 - dy)])
        for dx in range(3):
            col = 2 - dx
            both = got[0:128, 128 * col : 128 * (col + 1)] + got[128:256, 128 * (col + 1) : 128 * (col + 2)]
            where = slice(128 * (9 * dt + 3 * dy + dx), 128 * (9 * dt + 3 * dy + dx + 1))
            gk[where] = both if before is None else before[where] + both


def add_weights(gw, pairs, before):
    for n, (left, right) in enumerate(pairs):
        part = lax.dot_general(left[...], right[...], (((0,), (0,)), ((), ())), preferred_element_type=F32)
        where = slice(512 * n, 512 * (n + 1))
        gw[where] = part if before is None else before[where] + part


def early_kernel(lat, w1, w2, ker, act, slope, ft_a, cot_a, cot_b, *refs):
    part, gk, gw, act_b, slope_b, ft_b, taps, w1t, w2t, gm, gp, planes_a, planes_b, spread = refs
    n_px = gm.shape[0]
    mine = pl.ds(0, n_px)
    turn(w1, w2, ker, taps, w1t, w2t)
    split_all(cot_a, planes_a, spread)
    add_taps(gk, ft_a, 1, planes_a, None)
    split_all(cot_b, planes_b, spread)
    for k in range(ROWS // STEP):
        y = k * STEP
        total = own_cells(planes_a, y) + conv(taps, 1, planes_a, y) + conv(taps, 0, planes_b, y)
        gm[rows_of(k, STEP * 64)] = analyze(total)
    for k in range(ROWS // STEP):
        y = k * STEP
        part[rows_of(k, STEP * 128)] = own_cells(planes_b, y) + conv(taps, 1, planes_b, y)
    gp[...] = (dot(gm[...], w2t[...]) * slope[...].astype(F32)).astype(BF)
    add_weights(gw, ((lat.at[mine], gp), (act, gm)), None)
    project(lat[n_px : 2 * n_px], w1, w2, act_b, slope_b, ft_b)
    add_taps(gk, ft_a, 0, planes_b, None)
    add_taps(gk, ft_b, 1, planes_b, gk)


def late_kernel(lat, act, slope, ft, taps, w2t, cells, part, sumk, sumw, gm, gp, keep, send, *scratch):
    planes, spread, gk, gw = scratch
    n_px = gm.shape[0]
    mine = pl.ds(n_px, n_px)
    split_all(cells, planes, spread)

    for k in range(ROWS // STEP):
        total = part[rows_of(k, STEP * 128)] + conv(taps, 0, planes, k * STEP)
        gm[rows_of(k, STEP * 64)] = analyze(total)
    gp[...] = (dot(gm[...], w2t[...]) * slope[...].astype(F32)).astype(BF)
    add_taps(gk, ft, 0, planes, sumk)
    add_weights(gw, ((lat.at[mine], gp), (act, gm)), sumw)
    ids = block_ids()
    for r in range(8):
        packed = (keep, send)[r // 4].at[r % 4]
        b = ids[r]
        for lane in range(4):
            packed[128 * lane : 128 * (lane + 1), :] = gw[
                pl.ds(pl.multiple_of(b * 128, 128), 128), 128 * lane : 128 * (lane + 1)
            ].astype(BF)
        new = gk[pl.ds(pl.multiple_of((b % 4) * 288, 32), 288), :]
        old = sumk[pl.ds(pl.multiple_of(b * 288, 32), 288), :]
        packed[512:800, :] = jnp.where(b < 4, new, old).astype(BF)


def last_kernel(gm_a, gp_a, gm_b, gp_b, w1t, gl_h, gl, sems):
    n_px = gm_a.shape[0]
    copies = []
    for n, (gm, gp) in enumerate(((gm_a, gp_a), (gm_b, gp_b))):
        here = pl.ds(n * n_px, n_px)
        gl[here] = (gm[...].astype(F32) + dot(gp[...], w1t[...])).astype(BF)
        copies.append(pltpu.make_async_copy(gl.at[here], gl_h.at[here], sems.at[n]))
        copies[-1].start()
    for copy in copies:
        copy.wait()


PLANES = (ROWS + 2, 128, 512)
SUMS = [(2304, 128), (1024, 512)]
SPREAD = (2, 272, 128)


def early(lat, *rest):
    n_px = lat.shape[0] // 2
    ops = in_vmem(lat, *rest)
    shapes = [pltpu.VMEM(shape, F32) for shape in [(ROWS * 128, 256)] + SUMS]
    shapes += [pltpu.VMEM(shape, BF) for shape in frame_shapes(n_px) + [(6, 512, 256), (512, 512), (512, 512)]]
    shapes += [pltpu.VMEM((n_px, 512), BF)] * 2
    return pl.pallas_call(
        early_kernel,
        in_specs=[VMEM_SPEC] * len(ops),
        out_specs=[VMEM_SPEC] * len(shapes),
        out_shape=shapes,
        scratch_shapes=[pltpu.VMEM(PLANES, BF)] * 2
        + [pltpu.VMEM(SPREAD, F32)],
        cost_estimate=pl.CostEstimate(flops=12 << 30, bytes_accessed=16 * MIB, transcendentals=0),
        compiler_params=pltpu.CompilerParams(vmem_limit_bytes=24 * MIB),
    )(*ops)


def late(lat, act, slope, ft, taps, w2t, cells, part, gk, gw):
    half = (lat.shape[0] // 2, 512)
    ops = in_vmem(lat, act, slope, ft, taps, w2t, cells, part, gk, gw)
    return pl.pallas_call(
        late_kernel,
        in_specs=[VMEM_SPEC] * len(ops),
        out_specs=[VMEM_SPEC] * 4,
        out_shape=[pltpu.VMEM(half, BF)] * 2 + [pltpu.VMEM((4, 800, 128), BF)] * 2,
        scratch_shapes=[pltpu.VMEM(PLANES, BF), pltpu.VMEM(SPREAD, F32)]
        + [pltpu.VMEM(shape, F32) for shape in SUMS],
        cost_estimate=pl.CostEstimate(flops=6 << 30, bytes_accessed=16 * MIB, transcendentals=0),
        compiler_params=pltpu.CompilerParams(vmem_limit_bytes=24 * MIB),
    )(*ops)


def last(*ops):
    shape = (2 * ops[0].shape[0], 512)
    return pl.pallas_call(
        last_kernel,
        in_specs=[VMEM_SPEC] * 5,
        out_specs=ANY_SPEC,
        out_shape=pltpu.HBM(shape, BF),
        scratch_shapes=[pltpu.VMEM(shape, BF), pltpu.SemaphoreType.DMA((2,))],
        cost_estimate=pl.CostEstimate(flops=1 << 30, bytes_accessed=8 * MIB, transcendentals=0),
        compiler_params=pltpu.CompilerParams(vmem_limit_bytes=8 * MIB),
    )(*in_vmem(*ops))


def unpack_kernel(side, *refs):
    if side:
        (other, *_), refs = refs[:4], refs[4:]
        pieces = [other.at[r] for r in range(4)]
    else:
        pieces, refs = refs[:4], refs[4:]
    first_h, second_h, gk_h, gw, gk, sems = refs
    copies = []
    ids = block_ids()[4 * side : 4 * side + 4]
    for r in range(4):
        b, piece = ids[r], pieces[r]
        down = pl.ds(pl.multiple_of((b % 4) * 128, 128), 128)
        low = pl.ds(pl.multiple_of(b * 288, 32), 288)
        for lane in range(4):
            cols = slice(128 * lane, 128 * (lane + 1))
            gw[r, :, cols] = piece[cols, :].astype(F32)
        gk[r] = piece[512:800, :].astype(F32)
        copies.append(pltpu.make_async_copy(gk.at[r], gk_h.at[low], sems.at[0, r]))
        copies[-1].start()
        to_first = pltpu.make_async_copy(gw.at[r], first_h.at[down], sems.at[1, r])
        to_second = pltpu.make_async_copy(gw.at[r], second_h.at[down], sems.at[1, r])
        pl.when(b < 4)(to_first.start)
        pl.when(b >= 4)(to_second.start)
        copies.append(to_first)
    for copy in copies:
        copy.wait()


def unpack(side, pieces, outs=()):
    return pl.pallas_call(
        functools.partial(unpack_kernel, side),
        in_specs=[VMEM_SPEC] * len(pieces) + [ANY_SPEC] * len(outs),
        out_specs=[ANY_SPEC] * 3,
        out_shape=[pltpu.HBM(shape, F32) for shape in ((512, 512), (512, 512), (2304, 128))],
        input_output_aliases={1 + n: n for n in range(len(outs))},
        scratch_shapes=[
            pltpu.VMEM((4, 128, 512), F32),
            pltpu.VMEM((4, 288, 128), F32),
            pltpu.SemaphoreType.DMA((2, 4)),
        ],
        cost_estimate=pl.CostEstimate(flops=1 << 20, bytes_accessed=3 * MIB, transcendentals=0),
        compiler_params=pltpu.CompilerParams(vmem_limit_bytes=8 * MIB),
    )(*pieces, *in_hbm(*outs))


BOTH = ("ha", "ta")


def coords(device):
    ha, ta = divmod(device, 16)
    return [(ta // 2 % 2) * 2 + ha % 2, ha // 2, ta // 4, ta % 2]


def device_at(x, y, z, core):
    return (y * 2 + x % 2) * 16 + z * 4 + (x // 2) * 2 + core


def along(axes, move):
    pairs = []
    for device in range(128):
        place = coords(device)
        axis = axes[place[3]]
        place[axis] = move(place[axis])
        pairs.append((device, device_at(*place)))
    return pairs


def step_by(count):
    return lambda place: (place + count) % 4


def rounded(value):
    return lax.reduce_precision(value, 8, 7).astype(BF)


def swap(value):
    return lax.ppermute(value, BOTH, [(i, i ^ 1) for i in range(128)])


def trade(near, far, last, axes):
    across = lax.ppermute(far, BOTH, along(axes, step_by(2)))
    before = lax.ppermute(near, BOTH, along(axes, step_by(1)))
    after = lax.ppermute(last, BOTH, along(axes, step_by(3)))
    return before, across, after


def add4(own, before, across, after):
    return rounded((own.astype(F32) + across.astype(F32)) + (before.astype(F32) + after.astype(F32)))


def place():
    ha, ta = lax.axis_index("ha"), lax.axis_index("ta")
    return (ta // 2 % 2) * 2 + ha % 2, ha // 2, ta // 4, ta % 2


def block_ids():
    _, y, z, core = place()
    ids = []
    for other in range(2):
        owner = core ^ other
        start = jnp.where(owner == 0, z, y)
        ids += [owner * 4 + (start + k) % 4 for k in range(4)]
    return ids


def add2(a, b):
    return rounded(a.astype(F32) + b.astype(F32))


def sum_all(keep, got):
    parts = [add2(keep[k], got[k]) for k in range(4)]
    own = add4(parts[0], *trade(*parts[1:], (2, 1)))
    own = add4(own, *trade(own, own, own, (1, 0)))
    own = add4(own, *trade(own, own, own, (0, 2)))
    before, across, after = trade(own, own, own, (2, 1))
    other = swap(jnp.stack([own, after, across, before]))
    outs = unpack(0, (own, after, across, before))
    return unpack(1, (other,), outs)


def neighbour(value, axis, step):
    count = lax.axis_size(axis)
    return lax.ppermute(value, axis, [(i, i + step) for i in range(count) if 0 <= i + step < count])


def meetings(count):
    inner = [(i, i ^ 1) for i in range(count)]
    outer = [(i, i + 1 if i % 2 else i - 1) for i in range(1, count - 1)]
    return inner, outer


def shards(latent, w_first, w_second, kernel, cotangent):
    width = latent.shape[-1]
    flat = latent.reshape(-1, width)
    odd = lax.axis_index("ha") % 2
    top, bottom = cotangent[:, 0], cotangent[:, -1]
    meet = meetings(lax.axis_size("ha"))
    inner = lax.ppermute(jnp.where(odd == 1, top, bottom), "ha", meet[0])
    outer = lax.ppermute(jnp.where(odd == 1, bottom, top), "ha", meet[1])
    lat, w1, w2, ker, cot_a, cot_b, act_a, slope_a, ft_a = first(flat, w_first, w_second, kernel, cotangent)
    cot_a, cot_b = border(inner, outer, cot_a, cot_b)
    later = neighbour(cot_a, "ta", -1)
    middle = early(lat, w1, w2, ker, act_a, slope_a, ft_a, cot_a, cot_b)
    part, gk, gw, act_b, slope_b, ft_b, taps, w1t, w2t, gm_a, gp_a = middle
    gm, gp, keep, send = late(lat, act_b, slope_b, ft_b, taps, w2t, later, part, gk, gw)
    got = swap(send)
    grad = last(gm_a, gp_a, gm, gp, w1t)
    got, grad = lax.optimization_barrier((got, grad))
    grad_first, grad_second, gk = sum_all(keep, got)
    return grad.reshape(latent.shape), grad_first, grad_second, gk.reshape(kernel.shape)


def solution(mesh):
    return jax.shard_map(
        shards,
        mesh=mesh,
        in_specs=(P("ta", "ha", None, None), P(), P(), P(), P("ta", "ha", None, None)),
        out_specs=(P("ta", "ha", None, None), P(), P(), P()),
        check_vma=False,
    )
```
